512 devices in a mesh: seg: 32 (over z, y_lo), trait: 16 (over y_hi, x, core).
Axes of the slice: x: 4, y: 4 (y_hi: 2, y_lo: 2; y = y_hi * 2 + y_lo), z: 16, core: 2. Of those that a mesh axis runs over, the one named last changes fastest.
Arguments:
- effects: bfloat16 [16, 192, 32768], P(None, 'trait', 'seg'), may hold values from -6 to 6
- precision: float32 [192, 192], replicated, may hold values from -0.4375 to 0.4375
- band: bfloat16 [32768, 2048], P('seg'), may hold values from -0.15625 to 0.15625
Outputs:
- rhs: bfloat16 [16, 192, 32768], P(None, 'trait', 'seg')
The draws below stay inside these ranges and needn't reach their ends.
All inputs are finite; a program needn't handle non-finite values.
Results may differ from the reference program's by a relative error of at most 0.007.
Values may be sent and summed in bfloat16 or wider, within the bound.
No kernel may reach another device: no remote copies, remote signals or barrier semaphores. Data moves between devices by JAX's collectives and lax.ppermute only.
A program may use at most 64 MiB of HBM per device.

```python
import jax
import jax.numpy as jnp
from jax import lax

K = 192
W = 2048
MD = 1024
CH = 16
M = 32768


def shard_levels(rng, shape, pieces, least, largest):
    loudness = 1.0
    for dim, blocks in pieces:
        steps = jax.random.uniform(jax.random.fold_in(jax.random.fold_in(rng, 6), dim), (blocks,), jnp.float32, least / len(pieces), largest / len(pieces))
        loudness = loudness * jnp.repeat(jnp.exp(steps), shape[dim] // blocks).reshape((-1,) + (1,) * (len(shape) - 1 - dim))
    return loudness


def bell_draw(own_key, shape, spread, reach, split=(), kind=jnp.bfloat16):
    array = spread * jax.random.normal(own_key, shape, jnp.float32)
    if split:
        array = array * shard_levels(own_key, shape, split, -0.22, 0.18)
    return jnp.clip(array, -reach, reach).astype(kind)


def setup_inputs(seed: int = 0) -> dict:
    splits = jax.random.split(jax.random.key(seed), 4)
    effects = bell_draw(splits[0], (CH, K, M), 1.0, 6.0, ((1, 16), (2, 32)))
    precision = bell_draw(splits[1], (K, K), K ** -0.5, 0.4375, (), jnp.float32)
    band = bell_draw(splits[2], (M, W), (0.7 / (2 * W) ** 0.5), 0.15625, ((0, 32),))
    return dict(effects=effects, precision=precision, band=band)


def skew_band(rows):
    seg_rows, width = rows.shape
    padded = jnp.pad(rows, ((0, 0), (1, seg_rows)))
    span = width + 1 + seg_rows
    flat_band = padded.reshape(-1)[: seg_rows * (span - 1)]
    return flat_band.reshape(seg_rows, span - 1)


def reference(effects, precision, band):
    chains, traits, markers = effects.shape
    mixed = jnp.einsum("kj,ckm->cjm", precision, effects.astype(jnp.float32), precision=lax.Precision.HIGHEST).astype(jnp.bfloat16)
    columns = chains * traits
    mixed_rows = mixed.reshape(columns, markers)
    padded = jnp.pad(mixed_rows, ((0, 0), (0, W)))
    span = MD + W
    blocks = markers // MD

    def step(acc, block):
        start = (block * MD).astype(jnp.int32)
        zero = jnp.int32(0)
        rows = lax.dynamic_slice(band, (start, zero), (MD, W))
        dense = skew_band(rows)
        window = lax.dynamic_slice(padded, (zero, start), (columns, span))
        upper_part = lax.dot_general(window, dense, (((1,), (1,)), ((), ())), preferred_element_type=jnp.float32)
        lower_part = jnp.dot(window[:, :MD], dense, preferred_element_type=jnp.float32)
        lower_part = lower_part.at[:, :MD].add(upper_part)
        current = lax.dynamic_slice(acc, (zero, start), (columns, span))
        acc = lax.dynamic_update_slice(acc, current + lower_part, (zero, start))
        return acc, None

    init = jnp.zeros((columns, markers + W), jnp.float32)
    acc, _ = lax.scan(step, init, jnp.arange(blocks, dtype=jnp.int32))
    total = acc[:, :markers] + mixed_rows.astype(jnp.float32)
    return total.astype(jnp.bfloat16).reshape(chains, traits, markers)
```

```python
import jax
import jax.numpy as jnp
from jax import lax
from jax.experimental import pallas as pl
from jax.experimental.pallas import tpu as pltpu
from jax.sharding import PartitionSpec as P

F32 = jnp.float32
BF16 = jnp.bfloat16
LANES = 128
MIB = 1 << 20


def vmem_specs(count):
    return [pl.BlockSpec(memory_space=pltpu.VMEM)] * count


def params(mib):
    return pltpu.CompilerParams(vmem_limit_bytes=mib * MIB)


def pack_kernel(x_ref, o_ref, wide):
    m = x_ref.shape[1]
    blocks = m // LANES
    for k in range(blocks):
        wide[k] = x_ref[:, k * LANES : (k + 1) * LANES].astype(F32)
    for c in range(0, 16, 2):
        rows = pl.ds(8 * c, 16)
        for k in range(blocks):
            parts = [wide[k, pl.ds(d, 8, stride=16), :] for d in (c, c + 1)]
            o_ref[rows, k * LANES : (k + 1) * LANES] = jnp.concatenate(parts, 0).astype(BF16)
        for k in range(blocks // 2):
            parts = [
                wide[k + h, pl.ds(128 + d, 4, stride=16), :] for d in (c, c + 1) for h in (0, blocks // 2)
            ]
            o_ref[rows, m + k * LANES : m + (k + 1) * LANES] = jnp.concatenate(parts, 0).astype(BF16)


def unpack_kernel(x_ref, o_ref, wide):
    m = o_ref.shape[1]
    blocks = m // LANES
    for k in range(wide.shape[0]):
        wide[k] = x_ref[:, k * LANES : (k + 1) * LANES].astype(F32)
    for k in range(blocks):
        lanes = pl.ds(k * LANES, LANES)
        for j in range(8):
            o_ref[16 * j : 16 * j + 16, lanes] = wide[k, pl.ds(j, 16, stride=8), :].astype(BF16)
        half, place = divmod(k, blocks // 2)
        for j in range(4):
            tail = wide[blocks + place, pl.ds(j + 4 * half, 16, stride=8), :]
            o_ref[128 + 16 * j : 144 + 16 * j, lanes] = tail.astype(BF16)


def mix_kernel(x_ref, p_ref, o_ref):
    m = o_ref.shape[1]
    half = m // 2
    blank = jnp.zeros((4, p_ref.shape[1]), F32)
    heads, lows, highs = [], [], []
    for t in range(16):
        heads.append(p_ref[12 * t : 12 * t + 8, :])
        tail = p_ref[12 * t + 8 : 12 * t + 12, :]
        lows += [tail, blank]
        highs += [blank, tail]
    head = jnp.concatenate(heads, 0)
    for first, tails in ((0, lows), (half, highs)):
        weights = jnp.concatenate([head, jnp.concatenate(tails, 0)], 0).T
        upper = weights.astype(BF16)
        lower = (weights - upper.astype(F32)).astype(BF16)
        values = jnp.concatenate([x_ref[:, first : first + half], x_ref[:, m:]], 0)
        total = jnp.dot(upper, values, preferred_element_type=F32)
        total += jnp.dot(lower, values, preferred_element_type=F32)
        o_ref[:, first : first + half] = total.astype(BF16)


def skew_rows(band_ref, dense_ref, first):
    rows = pl.ds(first, LANES)
    blocks = band_ref.shape[1] // LANES
    a = lax.broadcasted_iota(jnp.int32, (LANES, LANES), 0)
    b = lax.broadcasted_iota(jnp.int32, (LANES, LANES), 1)
    beyond = b > a
    before = jnp.zeros((LANES, LANES), F32)
    for d in range(blocks + 1):
        if d < blocks:
            tile = band_ref[rows, d * LANES : (d + 1) * LANES].astype(F32)
            now = pltpu.roll(tile, 1, 1, stride=1, stride_axis=0)
        else:
            now = jnp.zeros((LANES, LANES), F32)
        dense_ref[rows, pl.ds(first + d * LANES, LANES)] = jnp.where(beyond, now, before).astype(BF16)
        before = now


def lower_kernel(x_ref, band_ref, dense_ref, own_ref, near_ref, far_ref):
    m, width = band_ref.shape
    depth = 256
    for first in range(0, m, LANES):
        skew_rows(band_ref, dense_ref, first)
        zero = jnp.zeros((LANES, LANES), BF16)
        if first % depth:
            dense_ref[pl.ds(first, LANES), pl.ds(first - LANES, LANES)] = zero
        else:
            dense_ref[pl.ds(first, LANES), pl.ds(first + width + LANES, LANES)] = zero
    for col in range(0, m + width, depth):
        low = max(0, col - width)
        high = min(m, col + depth)
        part = jnp.dot(
            x_ref[:, low:high], dense_ref[low:high, col : col + depth], preferred_element_type=F32
        )
        if col < m:
            own_ref[:, col : col + depth] = part + x_ref[:, col : col + depth].astype(F32)
        elif col < 2 * m:
            near_ref[:, col - m : col - m + depth] = part.astype(BF16)
        else:
            far_ref[:, col - 2 * m : col - 2 * m + depth] = part.astype(BF16)


def contract(values, dense):
    return lax.dot_general(values, dense, (((1,), (1,)), ((), ())), preferred_element_type=F32)


def upper_kernel(x_ref, near_ref, far_ref, dense_ref, own_ref, o_ref):
    rows, m = x_ref.shape
    depth = 256
    for i in range(0, m, depth):
        d = dense_ref.at[i : i + depth, :]
        total = own_ref[:, i : i + depth]
        total += contract(x_ref[:, i:], d[:, i:m])
        total += contract(near_ref[...], d[:, m : 2 * m])
        total += contract(far_ref[:, : i + depth], d[:, 2 * m : 2 * m + i + depth])
        o_ref[:, i : i + depth] = total


def finish_kernel(total_ref, near_ref, far_ref, o_ref, wide):
    m = total_ref.shape[1]
    half = m // 2
    wide[...] = total_ref[...] + near_ref[...].astype(F32) + far_ref[...].astype(F32)
    for t in range(0, 16, 2):
        parts = []
        for u in (t, t + 1):
            head = wide[12 * u : 12 * u + 8, :]
            left = wide[12 * u + 8 : 12 * u + 12, :half]
            right = wide[12 * u + 8 : 12 * u + 12, half:]
            parts.append(jnp.concatenate([head, jnp.concatenate([left, right], 0)], 1))
        o_ref[8 * t : 8 * t + 16, :] = jnp.concatenate(parts, 0).astype(BF16)


def call(kernel, name, outs, mib, *args, scratch=(), flops=0):
    several = isinstance(outs, tuple)
    size = sum(a.size * a.dtype.itemsize for a in args)
    return pl.pallas_call(
        kernel,
        out_shape=outs,
        in_specs=vmem_specs(len(args)),
        out_specs=tuple(vmem_specs(len(outs))) if several else vmem_specs(1)[0],
        scratch_shapes=list(scratch),
        compiler_params=params(mib),
        cost_estimate=pl.CostEstimate(flops=flops, bytes_accessed=size, transcendentals=0),
        name=name,
    )(*args)


def passed_along(shard, by):
    length = lax.axis_size("seg")
    pairs = [(i, i + by) for i in range(length) if 0 <= i + by < length]
    return lax.ppermute(shard, "seg", pairs)


def exchange(packed):
    rows, lanes = packed.shape
    moved = lax.all_to_all(packed.reshape(16, rows // 16, lanes), "trait", 0, 0, tiled=True)
    return moved.reshape(rows, lanes)


def local(effects, precision, band):
    chains, traits, m = effects.shape
    width = band.shape[1]
    rows = chains * traits
    packed_shape = (8 * chains, m + m // 2)
    struct = jax.ShapeDtypeStruct

    flat = effects.transpose(1, 0, 2).reshape(rows, m)
    packed = call(
        pack_kernel, "pack", struct(packed_shape, BF16), 8, flat,
        scratch=[pltpu.VMEM((m // LANES, rows, LANES), F32)],
    )
    mixed = call(mix_kernel, "mix", struct((rows, m), BF16), 8, exchange(packed), precision)
    far = passed_along(mixed, -2)
    near = passed_along(mixed, -1)
    dense, own, low_near, low_far = call(
        lower_kernel,
        "lower",
        (
            struct((m, m + width), BF16),
            struct((rows, m), F32),
            struct((rows, m), BF16),
            struct((rows, m), BF16),
        ),
        16,
        mixed,
        band,
        flops=2 * rows * m * width,
    )
    low_far = passed_along(low_far, 2)
    low_near = passed_along(low_near, 1)
    total = call(
        upper_kernel, "upper", struct((rows, m), F32), 16, mixed, near, far, dense, own,
        flops=2 * rows * m * width,
    )
    packed = call(
        finish_kernel, "finish", struct(packed_shape, BF16), 8, total, low_near, low_far,
        scratch=[pltpu.VMEM((rows, m), F32)],
    )
    flat = call(
        unpack_kernel, "unpack", struct((rows, m), BF16), 8, exchange(packed),
        scratch=[pltpu.VMEM((packed_shape[1] // LANES, packed_shape[0], LANES), F32)],
    )
    return flat.reshape(traits, chains, m).transpose(1, 0, 2)


def solution(mesh):
    in_specs = (P(None, "trait", "seg"), P(), P("seg", None))
    out_specs = P(None, "trait", "seg")
    return jax.shard_map(local, mesh=mesh, in_specs=in_specs, out_specs=out_specs, check_vma=False)
```

```python
import jax
import jax.numpy as jnp
from jax import lax
from jax.experimental import pallas as pl
from jax.experimental.pallas import tpu as pltpu
from jax.sharding import PartitionSpec as P

F32 = jnp.float32
BF16 = jnp.bfloat16
LANES = 128
MIB = 1 << 20


def vmem_specs(count):
    return [pl.BlockSpec(memory_space=pltpu.VMEM)] * count


def params(mib):
    return pltpu.CompilerParams(vmem_limit_bytes=mib * MIB)


def pack_kernel(x_ref, o_ref, near, wide, sems):
    rows, m = x_ref.shape
    blocks = m // LANES
    chunks = sems.shape[0]
    copies = []
    for q in range(chunks):
        lanes = pl.ds(q * (m // chunks), m // chunks)
        copies.append(pltpu.make_async_copy(x_ref.at[:, lanes], near.at[:, lanes], sems.at[q]))
        copies[-1].start()
    for q in range(chunks):
        copies[q].wait()
        for k in range(q * blocks // chunks, (q + 1) * blocks // chunks):
            wide[k] = near[:, k * LANES : (k + 1) * LANES].astype(F32)
            for c in range(0, 16, 2):
                parts = [wide[k, pl.ds(d, 8, stride=16), :] for d in (c, c + 1)]
                o_ref[8 * c : 8 * c + 16, k * LANES : (k + 1) * LANES] = jnp.concatenate(parts, 0).astype(BF16)
    for c in range(0, 16, 2):
        for k in range(blocks // 2):
            parts = [
                wide[k + h, pl.ds(128 + d, 4, stride=16), :] for d in (c, c + 1) for h in (0, blocks // 2)
            ]
            o_ref[8 * c : 8 * c + 16, m + k * LANES : m + (k + 1) * LANES] = jnp.concatenate(parts, 0).astype(BF16)


def unpack_kernel(x_ref, o_ref, wide):
    m = o_ref.shape[1]
    blocks = m // LANES
    for k in range(wide.shape[0]):
        wide[k] = x_ref[:, k * LANES : (k + 1) * LANES].astype(F32)
    for k in range(blocks):
        lanes = pl.ds(k * LANES, LANES)
        for j in range(8):
            o_ref[16 * j : 16 * j + 16, lanes] = wide[k, pl.ds(j, 16, stride=8), :].astype(BF16)
        half, place = divmod(k, blocks // 2)
        for j in range(4):
            tail = wide[blocks + place, pl.ds(j + 4 * half, 16, stride=8), :]
            o_ref[128 + 16 * j : 144 + 16 * j, lanes] = tail.astype(BF16)


def mix_kernel(x_ref, p_ref, dense_ref, o_ref, near_ref, far_ref, held, sems):
    m = o_ref.shape[1]
    half = m // 2
    width = dense_ref.shape[1] - m
    chunks = sems.shape[0]
    depth = width // chunks
    copies = []
    for k in range(chunks):
        low = max(0, m + k * depth - width)
        lanes = pl.ds(m + k * depth, depth)
        copy = pltpu.make_async_copy(
            dense_ref.at[low:, lanes], held.at[low:, k * depth : (k + 1) * depth], sems.at[k]
        )
        copy.start()
        copies.append((copy, low))
    blank = jnp.zeros((4, p_ref.shape[1]), F32)
    heads, lows, highs = [], [], []
    for t in range(16):
        heads.append(p_ref[12 * t : 12 * t + 8, :])
        tail = p_ref[12 * t + 8 : 12 * t + 12, :]
        lows += [tail, blank]
        highs += [blank, tail]
    head = jnp.concatenate(heads, 0)
    for first, tails in ((0, lows), (half, highs)):
        weights = jnp.concatenate([head, jnp.concatenate(tails, 0)], 0).T
        upper = weights.astype(BF16)
        lower = (weights - upper.astype(F32)).astype(BF16)
        values = jnp.concatenate([x_ref[:, first : first + half], x_ref[:, m:]], 0)
        total = jnp.dot(upper, values, preferred_element_type=F32)
        total += jnp.dot(lower, values, preferred_element_type=F32)
        o_ref[:, first : first + half] = total.astype(BF16)
    for k, (copy, _) in enumerate(copies):
        copy.wait()
        for col in range(k * depth, (k + 1) * depth, 256):
            low = max(0, m + col - width)
            part = jnp.dot(
                o_ref[:, low:], held[low:, col : col + 256], preferred_element_type=F32
            ).astype(BF16)
            if col < m:
                near_ref[:, col : col + 256] = part
            else:
                far_ref[:, col - m : col - m + 256] = part


def skew_rows(band_ref, dense_ref, first):
    rows = pl.ds(first, LANES)
    blocks = band_ref.shape[1] // LANES
    a = lax.broadcasted_iota(jnp.int32, (LANES, LANES), 0)
    b = lax.broadcasted_iota(jnp.int32, (LANES, LANES), 1)
    beyond = b > a
    before = jnp.zeros((LANES, LANES), F32)
    for d in range(blocks + 1):
        if d < blocks:
            tile = band_ref[rows, d * LANES : (d + 1) * LANES].astype(F32)
            now = pltpu.roll(tile, 1, 1, stride=1, stride_axis=0)
        else:
            now = jnp.zeros((LANES, LANES), F32)
        dense_ref[rows, pl.ds(first + d * LANES, LANES)] = jnp.where(beyond, now, before).astype(BF16)
        before = now


def skew_kernel(band_ref, dense_ref):
    m, width = band_ref.shape
    depth = 256
    for first in range(0, m, LANES):
        skew_rows(band_ref, dense_ref, first)
        zero = jnp.zeros((LANES, LANES), BF16)
        if first % depth:
            dense_ref[pl.ds(first, LANES), pl.ds(first - LANES, LANES)] = zero
        else:
            dense_ref[pl.ds(first, LANES), pl.ds(first + width + LANES, LANES)] = zero


def contract(values, dense):
    return lax.dot_general(values, dense, (((1,), (1,)), ((), ())), preferred_element_type=F32)


def own_kernel(x_ref, dense_ref, o_ref):
    m = x_ref.shape[1]
    depth = 256
    for i in range(0, m, depth):
        high = i + depth
        total = x_ref[:, i:high].astype(F32)
        total += jnp.dot(x_ref[:, :high], dense_ref[:high, i:high], preferred_element_type=F32)
        total += contract(x_ref[:, i:], dense_ref[i:high, i:m])
        o_ref[:, i:high] = total


def near_kernel(x_ref, low_ref, dense_ref, total_ref, o_ref):
    m = x_ref.shape[1]
    part = contract(x_ref[...], dense_ref[:, m : 2 * m])
    o_ref[...] = total_ref[...] + low_ref[...].astype(F32) + part


def far_kernel(x_ref, low_ref, dense_ref, total_ref, o_ref, wide):
    m = x_ref.shape[1]
    half = m // 2
    depth = 256
    for i in range(0, m, depth):
        high = i + depth
        part = contract(x_ref[:, :high], dense_ref[i:high, 2 * m : 2 * m + high])
        wide[:, i:high] = total_ref[:, i:high] + low_ref[:, i:high].astype(F32) + part
    for t in range(0, 16, 2):
        parts = []
        for u in (t, t + 1):
            head = wide[12 * u : 12 * u + 8, :]
            left = wide[12 * u + 8 : 12 * u + 12, :half]
            right = wide[12 * u + 8 : 12 * u + 12, half:]
            parts.append(jnp.concatenate([head, jnp.concatenate([left, right], 0)], 1))
        o_ref[8 * t : 8 * t + 16, :] = jnp.concatenate(parts, 0).astype(BF16)


def call(kernel, name, outs, mib, *args, scratch=(), flops=0, far_off=()):
    several = isinstance(outs, tuple)
    size = sum(a.size * a.dtype.itemsize for a in args)
    in_specs = vmem_specs(len(args))
    for k in far_off:
        in_specs[k] = pl.BlockSpec(memory_space=pltpu.HBM)
    return pl.pallas_call(
        kernel,
        out_shape=outs,
        in_specs=in_specs,
        out_specs=tuple(vmem_specs(len(outs))) if several else vmem_specs(1)[0],
        scratch_shapes=list(scratch),
        compiler_params=params(mib),
        cost_estimate=pl.CostEstimate(flops=flops, bytes_accessed=size, transcendentals=0),
        name=name,
    )(*args)


def passed_along(shard, by):
    length = lax.axis_size("seg")
    pairs = [(i, i + by) for i in range(length) if 0 <= i + by < length]
    return lax.ppermute(shard, "seg", pairs)


def exchange(packed):
    rows, lanes = packed.shape
    moved = lax.all_to_all(packed.reshape(16, rows // 16, lanes), "trait", 0, 0, tiled=True)
    return moved.reshape(rows, lanes)


def local(effects, precision, band):
    chains, traits, m = effects.shape
    width = band.shape[1]
    rows = chains * traits
    packed_shape = (8 * chains, m + m // 2)
    struct = jax.ShapeDtypeStruct

    flat = effects.transpose(1, 0, 2).reshape(rows, m)
    packed = call(
        pack_kernel, "pack", struct(packed_shape, BF16), 63, flat,
        far_off=(0,),
        scratch=[
            pltpu.VMEM((rows, m), BF16),
            pltpu.VMEM((m // LANES, rows, LANES), F32),
            pltpu.SemaphoreType.DMA((4,)),
        ],
    )
    dense = call(skew_kernel, "skew", struct((m, m + width), BF16), 16, band, flops=m * width)
    thin = struct((rows, m), BF16)
    mixed, low_near, low_far = call(
        mix_kernel, "mix", (thin, thin, thin), 52, exchange(packed), precision, dense,
        flops=2 * rows * m * width, far_off=(2,),
        scratch=[pltpu.VMEM((m, width), BF16), pltpu.SemaphoreType.DMA((4,))],
    )
    low_near = passed_along(low_near, 1)
    near = passed_along(mixed, -1)
    low_far = passed_along(low_far, 2)
    far = passed_along(mixed, -2)
    wide = struct((rows, m), F32)
    total = call(own_kernel, "own", wide, 16, mixed, dense, flops=4 * rows * m * m)
    total = call(near_kernel, "near", wide, 16, near, low_near, dense, total, flops=2 * rows * m * m)
    packed = call(
        far_kernel, "far", struct(packed_shape, BF16), 16, far, low_far, dense, total,
        flops=rows * m * m, scratch=[pltpu.VMEM((rows, m), F32)],
    )
    flat = call(
        unpack_kernel, "unpack", struct((rows, m), BF16), 8, exchange(packed),
        scratch=[pltpu.VMEM((packed_shape[1] // LANES, packed_shape[0], LANES), F32)],
    )
    return flat.reshape(traits, chains, m).transpose(1, 0, 2)


def solution(mesh):
    in_specs = (P(None, "trait", "seg"), P(), P("seg", None))
    out_specs = P(None, "trait", "seg")
    return jax.shard_map(local, mesh=mesh, in_specs=in_specs, out_specs=out_specs, check_vma=False)
```

```python
import jax
import jax.numpy as jnp
from jax import lax
from jax.experimental import pallas as pl
from jax.experimental.pallas import tpu as pltpu
from jax.sharding import PartitionSpec as P

F32 = jnp.float32
BF16 = jnp.bfloat16
LANES = 128
MIB = 1 << 20


def vmem_specs(count):
    return [pl.BlockSpec(memory_space=pltpu.VMEM)] * count


def params(mib):
    return pltpu.CompilerParams(vmem_limit_bytes=mib * MIB)


def swapped(place):
    return 8 * (place % 2) + 2 * (place // 2 % 4) + place // 8


def chain_places():
    odd = lax.rem(lax.axis_index("seg"), 2) == 1
    return [jnp.where(odd, swapped(p), p) for p in range(16)]


def pack_kernel(x_ref, o_ref, near, wide, packed, in_sems, out_sems):
    rows, m = x_ref.shape
    blocks = m // LANES
    chunks = in_sems.shape[0]
    part = m // chunks
    chains = chain_places()
    copies = []
    for q in range(chunks):
        lanes = pl.ds(q * part, part)
        copies.append(pltpu.make_async_copy(x_ref.at[:, lanes], near.at[:, lanes], in_sems.at[q]))
        copies[-1].start()
    out = []

    def send(first, size):
        lanes = pl.ds(first, size)
        out.append(pltpu.make_async_copy(packed.at[:, lanes], o_ref.at[:, lanes], out_sems.at[len(out)]))
        out[-1].start()

    for q in range(chunks):
        copies[q].wait()
        for k in range(q * blocks // chunks, (q + 1) * blocks // chunks):
            wide[k] = near[:, k * LANES : (k + 1) * LANES].astype(F32)
            for p in range(0, 16, 2):
                parts = [wide[k, pl.ds(d, 8, stride=16), :] for d in chains[p : p + 2]]
                packed[8 * p : 8 * p + 16, k * LANES : (k + 1) * LANES] = jnp.concatenate(parts, 0).astype(BF16)
        send(q * part, part)
    for p in range(0, 16, 2):
        for k in range(blocks // 2):
            parts = [
                wide[k + h, pl.ds(128 + d, 4, stride=16), :]
                for d in chains[p : p + 2]
                for h in (0, blocks // 2)
            ]
            packed[8 * p : 8 * p + 16, m + k * LANES : m + (k + 1) * LANES] = jnp.concatenate(parts, 0).astype(BF16)
    send(m, m // 2)
    for copy in out:
        copy.wait()


def unpack_kernel(x_ref, o_ref, wide):
    m = o_ref.shape[1]
    blocks = m // LANES
    chains = chain_places()
    for k in range(wide.shape[0]):
        for p in range(0, 16, 2):
            pair = x_ref[8 * p : 8 * p + 16, k * LANES : (k + 1) * LANES].astype(F32)
            for h in range(2):
                wide[k, pl.ds(pl.multiple_of(8 * chains[p + h], 8), 8), :] = pair[8 * h : 8 * h + 8]
    for k in range(blocks):
        lanes = pl.ds(k * LANES, LANES)
        for j in range(8):
            o_ref[16 * j : 16 * j + 16, lanes] = wide[k, pl.ds(j, 16, stride=8), :].astype(BF16)
        half, place = divmod(k, blocks // 2)
        for j in range(4):
            tail = wide[blocks + place, pl.ds(j + 4 * half, 16, stride=8), :]
            o_ref[128 + 16 * j : 144 + 16 * j, lanes] = tail.astype(BF16)


def mix_kernel(x_ref, p_ref, beyond_ref, o_ref, near_ref, far_ref, held, sems):
    m = o_ref.shape[1]
    half = m // 2
    width = beyond_ref.shape[1]
    chunks = sems.shape[0]
    depth = width // chunks
    copies = []
    for k in range(chunks):
        low = max(0, m + k * depth - width)
        lanes = pl.ds(k * depth, depth)
        copies.append(pltpu.make_async_copy(beyond_ref.at[low:, lanes], held.at[low:, lanes], sems.at[k]))
        copies[-1].start()
    blank = jnp.zeros((4, p_ref.shape[1]), F32)
    heads, lows, highs = [], [], []
    for t in range(16):
        heads.append(p_ref[12 * t : 12 * t + 8, :])
        tail = p_ref[12 * t + 8 : 12 * t + 12, :]
        lows += [tail, blank]
        highs += [blank, tail]
    head = jnp.concatenate(heads, 0)
    for first, tails in ((0, lows), (half, highs)):
        weights = jnp.concatenate([head, jnp.concatenate(tails, 0)], 0).T
        upper = weights.astype(BF16)
        lower = (weights - upper.astype(F32)).astype(BF16)
        values = jnp.concatenate([x_ref[:, first : first + half], x_ref[:, m:]], 0)
        total = jnp.dot(upper, values, preferred_element_type=F32)
        total += jnp.dot(lower, values, preferred_element_type=F32)
        o_ref[:, first : first + half] = total.astype(BF16)
    for k, copy in enumerate(copies):
        copy.wait()
        for col in range(k * depth, (k + 1) * depth, 256):
            low = max(0, m + col - width)
            part = jnp.dot(
                o_ref[:, low:], held[low:, col : col + 256], preferred_element_type=F32
            ).astype(BF16)
            if col < m:
                near_ref[:, col : col + 256] = part
            else:
                far_ref[:, col - m : col - m + 256] = part


def skew_rows(band_ref, own_ref, beyond_ref, first):
    m, width = band_ref.shape
    rows = pl.ds(first, LANES)

    def put(col, tile):
        if col < m:
            own_ref[rows, pl.ds(col, LANES)] = tile
        elif col < m + width:
            beyond_ref[rows, pl.ds(col - m, LANES)] = tile

    a = lax.broadcasted_iota(jnp.int32, (LANES, LANES), 0)
    b = lax.broadcasted_iota(jnp.int32, (LANES, LANES), 1)
    ahead = b > a
    zero = jnp.zeros((LANES, LANES), F32)
    before = zero
    for d in range(width // LANES + 1):
        if d < width // LANES:
            tile = band_ref[rows, d * LANES : (d + 1) * LANES].astype(F32)
            now = pltpu.roll(tile, 1, 1, stride=1, stride_axis=0)
        else:
            now = zero
        put(first + d * LANES, jnp.where(ahead, now, before).astype(BF16))
        before = now
    if first % 256:
        put(first - LANES, zero.astype(BF16))
    else:
        put(first + width + LANES, zero.astype(BF16))


def skew_kernel(band_ref, own_ref, beyond_ref):
    for first in range(0, band_ref.shape[0], LANES):
        skew_rows(band_ref, own_ref, beyond_ref, first)


def contract(values, dense):
    return lax.dot_general(values, dense, (((1,), (1,)), ((), ())), preferred_element_type=F32)


def own_kernel(x_ref, dense_ref, o_ref):
    m = x_ref.shape[1]
    depth = 256
    for i in range(0, m, depth):
        high = i + depth
        total = x_ref[:, i:high].astype(F32)
        total += jnp.dot(x_ref[:, :high], dense_ref[:high, i:high], preferred_element_type=F32)
        total += contract(x_ref[:, i:], dense_ref[i:high, i:m])
        o_ref[:, i:high] = total


def near_kernel(x_ref, low_ref, dense_ref, total_ref, o_ref):
    m = x_ref.shape[1]
    part = contract(x_ref[...], dense_ref[:, :m])
    o_ref[...] = total_ref[...] + low_ref[...].astype(F32) + part


def far_kernel(x_ref, low_ref, dense_ref, total_ref, o_ref, wide):
    m = x_ref.shape[1]
    half = m // 2
    depth = 256
    for i in range(0, m, depth):
        high = i + depth
        part = contract(x_ref[:, :high], dense_ref[i:high, m : m + high])
        wide[:, i:high] = total_ref[:, i:high] + low_ref[:, i:high].astype(F32) + part
    for t in range(0, 16, 2):
        parts = []
        for u in (t, t + 1):
            head = wide[12 * u : 12 * u + 8, :]
            left = wide[12 * u + 8 : 12 * u + 12, :half]
            right = wide[12 * u + 8 : 12 * u + 12, half:]
            parts.append(jnp.concatenate([head, jnp.concatenate([left, right], 0)], 1))
        o_ref[8 * t : 8 * t + 16, :] = jnp.concatenate(parts, 0).astype(BF16)


def call(kernel, name, outs, mib, *args, scratch=(), flops=0, far_off=(), far_out=False):
    several = isinstance(outs, tuple)
    size = sum(a.size * a.dtype.itemsize for a in args)
    in_specs = vmem_specs(len(args))
    for k in far_off:
        in_specs[k] = pl.BlockSpec(memory_space=pltpu.HBM)
    out_spec = pl.BlockSpec(memory_space=pltpu.HBM if far_out else pltpu.VMEM)
    return pl.pallas_call(
        kernel,
        out_shape=outs,
        in_specs=in_specs,
        out_specs=tuple(vmem_specs(len(outs))) if several else out_spec,
        scratch_shapes=list(scratch),
        compiler_params=params(mib),
        cost_estimate=pl.CostEstimate(flops=flops, bytes_accessed=size, transcendentals=0),
        name=name,
    )(*args)


def passed_along(shard, by):
    length, places = lax.axis_size("seg"), lax.axis_size("trait")
    pairs = []
    for s in range(length):
        for p in range(places):
            if 0 <= s + by < length:
                pairs.append((s * places + p, (s + by) * places + (swapped(p) if by % 2 else p)))
    return lax.ppermute(shard, ("seg", "trait"), pairs)


def exchange(packed):
    rows, lanes = packed.shape
    moved = lax.all_to_all(packed.reshape(16, rows // 16, lanes), "trait", 0, 0, tiled=True)
    return moved.reshape(rows, lanes)


def local(effects, precision, band):
    chains, traits, m = effects.shape
    width = band.shape[1]
    rows = chains * traits
    packed_shape = (8 * chains, m + m // 2)
    struct = jax.ShapeDtypeStruct

    flat = effects.transpose(1, 0, 2).reshape(rows, m)
    packed = call(
        pack_kernel, "pack", struct(packed_shape, BF16), 63, flat,
        far_off=(0,), far_out=True,
        scratch=[
            pltpu.VMEM((rows, m), BF16),
            pltpu.VMEM((m // LANES, rows, LANES), F32),
            pltpu.VMEM(packed_shape, BF16),
            pltpu.SemaphoreType.DMA((4,)),
            pltpu.SemaphoreType.DMA((5,)),
        ],
    )
    within, beyond = call(
        skew_kernel, "skew", (struct((m, m), BF16), struct((m, width), BF16)), 16, band, flops=m * width
    )
    thin = struct((rows, m), BF16)
    mixed, low_near, low_far, beyond = call(
        mix_kernel, "mix", (thin, thin, thin, struct((m, width), BF16)), 48,
        exchange(packed), precision, beyond,
        flops=2 * rows * m * width, far_off=(2,),
        scratch=[pltpu.SemaphoreType.DMA((4,))],
    )
    low_near = passed_along(low_near, 1)
    near = passed_along(mixed, -1)
    low_far = passed_along(low_far, 2)
    far = passed_along(mixed, -2)
    wide = struct((rows, m), F32)
    total = call(own_kernel, "own", wide, 16, mixed, within, flops=4 * rows * m * m)
    total = call(near_kernel, "near", wide, 16, near, low_near, beyond, total, flops=2 * rows * m * m)
    packed = call(
        far_kernel, "far", struct(packed_shape, BF16), 16, far, low_far, beyond, total,
        flops=rows * m * m, scratch=[pltpu.VMEM((rows, m), F32)],
    )
    flat = call(
        unpack_kernel, "unpack", struct((rows, m), BF16), 8, exchange(packed),
        scratch=[pltpu.VMEM((packed_shape[1] // LANES, packed_shape[0], LANES), F32)],
    )
    return flat.reshape(traits, chains, m).transpose(1, 0, 2)


def solution(mesh):
    in_specs = (P(None, "trait", "seg"), P(), P("seg", None))
    out_specs = P(None, "trait", "seg")
    return jax.shard_map(local, mesh=mesh, in_specs=in_specs, out_specs=out_specs, check_vma=False)
```

```python
import jax
import jax.numpy as jnp
from jax import lax
from jax.experimental import pallas as pl
from jax.experimental.pallas import tpu as pltpu
from jax.sharding import PartitionSpec as P

F32 = jnp.float32
BF16 = jnp.bfloat16
LANES = 128
MIB = 1 << 20


def vmem_specs(count):
    return [pl.BlockSpec(memory_space=pltpu.VMEM)] * count


def params(mib):
    return pltpu.CompilerParams(vmem_limit_bytes=mib * MIB)


def swapped(place):
    return 8 * (place % 2) + 2 * (place // 2 % 4) + place // 8


def chain_places():
    odd = lax.rem(lax.axis_index("seg"), 2) == 1
    return [jnp.where(odd, swapped(p), p) for p in range(16)]


def pack_kernel(x_ref, o_ref, near, wide, packed, in_sems, out_sems):
    rows, m = x_ref.shape
    blocks = m // LANES
    chunks = in_sems.shape[0]
    part = m // chunks
    chains = chain_places()
    copies = []
    for q in range(chunks):
        lanes = pl.ds(q * part, part)
        copies.append(pltpu.make_async_copy(x_ref.at[:, lanes], near.at[:, lanes], in_sems.at[q]))
        copies[-1].start()
    out = []

    def send(first, size):
        lanes = pl.ds(first, size)
        out.append(pltpu.make_async_copy(packed.at[:, lanes], o_ref.at[:, lanes], out_sems.at[len(out)]))
        out[-1].start()

    for q in range(chunks):
        copies[q].wait()
        for k in range(q * blocks // chunks, (q + 1) * blocks // chunks):
            wide[k] = near[:, k * LANES : (k + 1) * LANES].astype(F32)
            for p in range(0, 16, 2):
                parts = [wide[k, pl.ds(d, 8, stride=16), :] for d in chains[p : p + 2]]
                packed[8 * p : 8 * p + 16, k * LANES : (k + 1) * LANES] = jnp.concatenate(parts, 0).astype(BF16)
        send(q * part, part)
    for p in range(0, 16, 2):
        for k in range(blocks // 2):
            parts = [
                wide[k + h, pl.ds(128 + d, 4, stride=16), :]
                for d in chains[p : p + 2]
                for h in (0, blocks // 2)
            ]
            packed[8 * p : 8 * p + 16, m + k * LANES : m + (k + 1) * LANES] = jnp.concatenate(parts, 0).astype(BF16)
    send(m, m // 2)
    for copy in out:
        copy.wait()


def unpack_kernel(x_ref, o_ref, wide):
    m = o_ref.shape[1]
    blocks = m // LANES
    chains = chain_places()
    for k in range(wide.shape[0]):
        for p in range(0, 16, 2):
            pair = x_ref[8 * p : 8 * p + 16, k * LANES : (k + 1) * LANES].astype(F32)
            for h in range(2):
                wide[k, pl.ds(pl.multiple_of(8 * chains[p + h], 8), 8), :] = pair[8 * h : 8 * h + 8]
    for k in range(blocks):
        lanes = pl.ds(k * LANES, LANES)
        for j in range(8):
            o_ref[16 * j : 16 * j + 16, lanes] = wide[k, pl.ds(j, 16, stride=8), :].astype(BF16)
        half, place = divmod(k, blocks // 2)
        for j in range(4):
            tail = wide[blocks + place, pl.ds(j + 4 * half, 16, stride=8), :]
            o_ref[128 + 16 * j : 144 + 16 * j, lanes] = tail.astype(BF16)


def mix_kernel(x_ref, p_ref, o_ref):
    m = o_ref.shape[1]
    half = m // 2
    blank = jnp.zeros((4, p_ref.shape[1]), F32)
    heads, lows, highs = [], [], []
    for t in range(16):
        heads.append(p_ref[12 * t : 12 * t + 8, :])
        tail = p_ref[12 * t + 8 : 12 * t + 12, :]
        lows += [tail, blank]
        highs += [blank, tail]
    head = jnp.concatenate(heads, 0)
    for first, tails in ((0, lows), (half, highs)):
        weights = jnp.concatenate([head, jnp.concatenate(tails, 0)], 0).T
        upper = weights.astype(BF16)
        lower = (weights - upper.astype(F32)).astype(BF16)
        values = jnp.concatenate([x_ref[:, first : first + half], x_ref[:, m:]], 0)
        total = jnp.dot(upper, values, preferred_element_type=F32)
        total += jnp.dot(lower, values, preferred_element_type=F32)
        o_ref[:, first : first + half] = total.astype(BF16)

def lower_near_kernel(x_ref, dense_ref, o_ref):
    o_ref[...] = jnp.dot(x_ref[...], dense_ref[...], preferred_element_type=F32).astype(BF16)


def lower_far_kernel(x_ref, dense_ref, o_ref):
    depth = 256
    for i in range(0, x_ref.shape[1], depth):
        part = jnp.dot(x_ref[:, i:], dense_ref[i:, i : i + depth], preferred_element_type=F32)
        o_ref[:, i : i + depth] = part.astype(BF16)


def skew_rows(band_ref, dense_refs, first):
    m, width = band_ref.shape
    rows = pl.ds(first, LANES)

    def put(col, tile):
        if col < m + width:
            dense_refs[col // m][rows, pl.ds(col % m, LANES)] = tile

    a = lax.broadcasted_iota(jnp.int32, (LANES, LANES), 0)
    b = lax.broadcasted_iota(jnp.int32, (LANES, LANES), 1)
    ahead = b > a
    zero = jnp.zeros((LANES, LANES), F32)
    before = zero
    for d in range(width // LANES + 1):
        if d < width // LANES:
            tile = band_ref[rows, d * LANES : (d + 1) * LANES].astype(F32)
            now = pltpu.roll(tile, 1, 1, stride=1, stride_axis=0)
        else:
            now = zero
        put(first + d * LANES, jnp.where(ahead, now, before).astype(BF16))
        before = now
    if first % 256:
        put(first - LANES, zero.astype(BF16))
    else:
        put(first + width + LANES, zero.astype(BF16))


def skew_kernel(band_ref, *dense_refs):
    for first in range(0, band_ref.shape[0], LANES):
        skew_rows(band_ref, dense_refs, first)


def contract(values, dense):
    return lax.dot_general(values, dense, (((1,), (1,)), ((), ())), preferred_element_type=F32)


def own_kernel(x_ref, dense_ref, o_ref):
    m = x_ref.shape[1]
    depth = 256
    for i in range(0, m, depth):
        high = i + depth
        total = x_ref[:, i:high].astype(F32)
        total += jnp.dot(x_ref[:, :high], dense_ref[:high, i:high], preferred_element_type=F32)
        total += contract(x_ref[:, i:], dense_ref[i:high, i:m])
        o_ref[:, i:high] = total


def far_kernel(x_ref, dense_ref, total_ref, o_ref):
    m = x_ref.shape[1]
    depth = 256
    for i in range(0, m, depth):
        high = i + depth
        o_ref[:, i:high] = total_ref[:, i:high] + contract(x_ref[:, :high], dense_ref[i:high, :high])


def near_kernel(x_ref, low_near_ref, low_far_ref, dense_ref, total_ref, o_ref, wide):
    m = x_ref.shape[1]
    half = m // 2
    wide[...] = total_ref[...] + low_near_ref[...].astype(F32) + low_far_ref[...].astype(F32)
    wide[...] += contract(x_ref[...], dense_ref[...])
    for t in range(0, 16, 2):
        parts = []
        for u in (t, t + 1):
            head = wide[12 * u : 12 * u + 8, :]
            left = wide[12 * u + 8 : 12 * u + 12, :half]
            right = wide[12 * u + 8 : 12 * u + 12, half:]
            parts.append(jnp.concatenate([head, jnp.concatenate([left, right], 0)], 1))
        o_ref[8 * t : 8 * t + 16, :] = jnp.concatenate(parts, 0).astype(BF16)


def call(kernel, name, outs, mib, *args, scratch=(), flops=0, far_off=(), far_out=False):
    several = isinstance(outs, tuple)
    size = sum(a.size * a.dtype.itemsize for a in args)
    in_specs = vmem_specs(len(args))
    for k in far_off:
        in_specs[k] = pl.BlockSpec(memory_space=pltpu.HBM)
    out_spec = pl.BlockSpec(memory_space=pltpu.HBM if far_out else pltpu.VMEM)
    return pl.pallas_call(
        kernel,
        out_shape=outs,
        in_specs=in_specs,
        out_specs=tuple(vmem_specs(len(outs))) if several else out_spec,
        scratch_shapes=list(scratch),
        compiler_params=params(mib),
        cost_estimate=pl.CostEstimate(flops=flops, bytes_accessed=size, transcendentals=0),
        name=name,
    )(*args)


def passed_along(shard, by):
    length, places = lax.axis_size("seg"), lax.axis_size("trait")
    pairs = []
    for s in range(length):
        for p in range(places):
            if 0 <= s + by < length:
                pairs.append((s * places + p, (s + by) * places + (swapped(p) if by % 2 else p)))
    return lax.ppermute(shard, ("seg", "trait"), pairs)


def traded(shard):
    length, places = lax.axis_size("seg"), lax.axis_size("trait")
    pairs = [(s * places + p, (s ^ 1) * places + swapped(p)) for s in range(length) for p in range(places)]
    return lax.ppermute(shard, ("seg", "trait"), pairs)


def exchange(packed):
    rows, lanes = packed.shape
    moved = lax.all_to_all(packed.reshape(16, rows // 16, lanes), "trait", 0, 0, tiled=True)
    return moved.reshape(rows, lanes)


def local(effects, precision, band):
    chains, traits, m = effects.shape
    width = band.shape[1]
    rows = chains * traits
    packed_shape = (8 * chains, m + m // 2)
    struct = jax.ShapeDtypeStruct

    flat = effects.transpose(1, 0, 2).reshape(rows, m)
    packed = call(
        pack_kernel, "pack", struct(packed_shape, BF16), 63, flat,
        far_off=(0,), far_out=True,
        scratch=[
            pltpu.VMEM((rows, m), BF16),
            pltpu.VMEM((m // LANES, rows, LANES), F32),
            pltpu.VMEM(packed_shape, BF16),
            pltpu.SemaphoreType.DMA((4,)),
            pltpu.SemaphoreType.DMA((5,)),
        ],
    )
    square = struct((m, m), BF16)
    within, following, last = call(
        skew_kernel, "skew", (square, square, square), 16, band, flops=m * width
    )
    thin = struct((rows, m), BF16)
    gathered, following = lax.optimization_barrier((exchange(packed), following))
    mixed = call(mix_kernel, "mix", thin, 16, gathered, precision, flops=4 * rows * rows * m)
    far = passed_along(mixed, -2)
    low_near = call(lower_near_kernel, "lower_near", thin, 16, mixed, following, flops=2 * rows * m * m)
    low_near = passed_along(low_near, 1)
    low_far = call(lower_far_kernel, "lower_far", thin, 16, mixed, last, flops=rows * m * m)
    low_far = passed_along(low_far, 2)
    odd = lax.axis_index("seg") % 2 == 1
    near = traded(jnp.where(odd, mixed, far))
    wide = struct((rows, m), F32)
    total = call(own_kernel, "own", wide, 16, mixed, within, flops=4 * rows * m * m)
    total = call(far_kernel, "far", wide, 16, far, last, total, flops=rows * m * m)
    packed = call(
        near_kernel, "near", struct(packed_shape, BF16), 16, near, low_near, low_far, following, total,
        flops=2 * rows * m * m, scratch=[pltpu.VMEM((rows, m), F32)],
    )
    flat = call(
        unpack_kernel, "unpack", struct((rows, m), BF16), 8, exchange(packed),
        scratch=[pltpu.VMEM((packed_shape[1] // LANES, packed_shape[0], LANES), F32)],
    )
    return flat.reshape(traits, chains, m).transpose(1, 0, 2)


def solution(mesh):
    in_specs = (P(None, "trait", "seg"), P(), P("seg", None))
    out_specs = P(None, "trait", "seg")
    return jax.shard_map(local, mesh=mesh, in_specs=in_specs, out_specs=out_specs, check_vma=False)
```

```python
import jax
import jax.numpy as jnp
from jax import lax
from jax.experimental import pallas as pl
from jax.experimental.pallas import tpu as pltpu
from jax.sharding import PartitionSpec as P

F32 = jnp.float32
BF16 = jnp.bfloat16
LANES = 128
MIB = 1 << 20


def vmem_specs(count):
    return [pl.BlockSpec(memory_space=pltpu.VMEM)] * count


def params(mib):
    return pltpu.CompilerParams(vmem_limit_bytes=mib * MIB)


def swapped(place):
    return 8 * (place % 2) + 2 * (place // 2 % 4) + place // 8


def chain_places():
    odd = lax.rem(lax.axis_index("seg"), 2) == 1
    return [jnp.where(odd, swapped(p), p) for p in range(16)]


def pack_kernel(x_ref, o_ref, near, wide, packed, in_sems, out_sems):
    rows, m = x_ref.shape
    blocks = m // LANES
    chunks = in_sems.shape[0]
    part = m // chunks
    chains = chain_places()
    copies = []
    for q in range(chunks):
        lanes = pl.ds(q * part, part)
        copies.append(pltpu.make_async_copy(x_ref.at[:, lanes], near.at[:, lanes], in_sems.at[q]))
        copies[-1].start()
    out = []

    def send(first, size):
        lanes = pl.ds(first, size)
        out.append(pltpu.make_async_copy(packed.at[:, lanes], o_ref.at[:, lanes], out_sems.at[len(out)]))
        out[-1].start()

    for q in range(chunks):
        copies[q].wait()
        for k in range(q * blocks // chunks, (q + 1) * blocks // chunks):
            wide[k] = near[:, k * LANES : (k + 1) * LANES].astype(F32)
            for p in range(0, 16, 2):
                parts = [wide[k, pl.ds(d, 8, stride=16), :] for d in chains[p : p + 2]]
                packed[8 * p : 8 * p + 16, k * LANES : (k + 1) * LANES] = jnp.concatenate(parts, 0).astype(BF16)
        send(q * part, part)
    for p in range(0, 16, 2):
        for k in range(blocks // 2):
            parts = [
                wide[k + h, pl.ds(128 + d, 4, stride=16), :]
                for d in chains[p : p + 2]
                for h in (0, blocks // 2)
            ]
            packed[8 * p : 8 * p + 16, m + k * LANES : m + (k + 1) * LANES] = jnp.concatenate(parts, 0).astype(BF16)
    send(m, m // 2)
    for copy in out:
        copy.wait()


def unpack_kernel(x_ref, o_ref, wide):
    m = o_ref.shape[1]
    blocks = m // LANES
    chains = chain_places()
    for k in range(wide.shape[0]):
        for p in range(0, 16, 2):
            pair = x_ref[8 * p : 8 * p + 16, k * LANES : (k + 1) * LANES].astype(F32)
            for h in range(2):
                wide[k, pl.ds(pl.multiple_of(8 * chains[p + h], 8), 8), :] = pair[8 * h : 8 * h + 8]
    for k in range(blocks):
        lanes = pl.ds(k * LANES, LANES)
        for j in range(8):
            o_ref[16 * j : 16 * j + 16, lanes] = wide[k, pl.ds(j, 16, stride=8), :].astype(BF16)
        half, place = divmod(k, blocks // 2)
        for j in range(4):
            tail = wide[blocks + place, pl.ds(j + 4 * half, 16, stride=8), :]
            o_ref[128 + 16 * j : 144 + 16 * j, lanes] = tail.astype(BF16)


def mix_kernel(x_ref, p_ref, o_ref):
    m = o_ref.shape[1]
    half = m // 2
    blank = jnp.zeros((4, p_ref.shape[1]), F32)
    heads, lows, highs = [], [], []
    for t in range(16):
        heads.append(p_ref[12 * t : 12 * t + 8, :])
        tail = p_ref[12 * t + 8 : 12 * t + 12, :]
        lows += [tail, blank]
        highs += [blank, tail]
    head = jnp.concatenate(heads, 0)
    for first, tails in ((0, lows), (half, highs)):
        weights = jnp.concatenate([head, jnp.concatenate(tails, 0)], 0).T
        upper = weights.astype(BF16)
        lower = (weights - upper.astype(F32)).astype(BF16)
        values = jnp.concatenate([x_ref[:, first : first + half], x_ref[:, m:]], 0)
        total = jnp.dot(upper, values, preferred_element_type=F32)
        total += jnp.dot(lower, values, preferred_element_type=F32)
        o_ref[:, first : first + half] = total.astype(BF16)

def lower_near_kernel(x_ref, dense_ref, o_ref):
    o_ref[...] = jnp.dot(x_ref[...], dense_ref[...], preferred_element_type=F32).astype(BF16)


def lower_far_kernel(x_ref, dense_ref, o_ref):
    depth = 256
    for i in range(0, x_ref.shape[1], depth):
        part = jnp.dot(x_ref[:, i:], dense_ref[i:, i : i + depth], preferred_element_type=F32)
        o_ref[:, i : i + depth] = part


def skew_rows(band_ref, dense_refs, first):
    m, width = band_ref.shape
    rows = pl.ds(first, LANES)

    def put(col, tile):
        if col < m + width:
            dense_refs[col // m][rows, pl.ds(col % m, LANES)] = tile

    a = lax.broadcasted_iota(jnp.int32, (LANES, LANES), 0)
    b = lax.broadcasted_iota(jnp.int32, (LANES, LANES), 1)
    ahead = b > a
    zero = jnp.zeros((LANES, LANES), F32)
    before = zero
    for d in range(width // LANES + 1):
        if d < width // LANES:
            tile = band_ref[rows, d * LANES : (d + 1) * LANES].astype(F32)
            now = pltpu.roll(tile, 1, 1, stride=1, stride_axis=0)
        else:
            now = zero
        put(first + d * LANES, jnp.where(ahead, now, before).astype(BF16))
        before = now
    if first % 256:
        put(first - LANES, zero.astype(BF16))
    else:
        put(first + width + LANES, zero.astype(BF16))


def skew_kernel(band_ref, *dense_refs):
    for first in range(0, band_ref.shape[0], LANES):
        skew_rows(band_ref, dense_refs, first)


def on_odd_segment():
    return lax.rem(lax.axis_index("seg"), 2) == 1


def join_kernel(far_ref, near_ref, o_ref):
    near = near_ref[...].astype(F32)
    o_ref[...] = (far_ref[...] + jnp.where(on_odd_segment(), jnp.zeros_like(near), near)).astype(BF16)


def choose_kernel(own_ref, far_ref, o_ref):
    @pl.when(on_odd_segment())
    def _():
        o_ref[...] = own_ref[...]

    @pl.when(jnp.logical_not(on_odd_segment()))
    def _():
        o_ref[...] = far_ref[...]


def contract(values, dense):
    return lax.dot_general(values, dense, (((1,), (1,)), ((), ())), preferred_element_type=F32)


def own_kernel(x_ref, dense_ref, o_ref):
    m = x_ref.shape[1]
    depth = 256
    for i in range(0, m, depth):
        high = i + depth
        total = x_ref[:, i:high].astype(F32)
        total += jnp.dot(x_ref[:, :high], dense_ref[:high, i:high], preferred_element_type=F32)
        total += contract(x_ref[:, i:], dense_ref[i:high, i:m])
        o_ref[:, i:high] = total


def far_kernel(x_ref, dense_ref, total_ref, o_ref):
    m = x_ref.shape[1]
    depth = 256
    for i in range(0, m, depth):
        high = i + depth
        o_ref[:, i:high] = total_ref[:, i:high] + contract(x_ref[:, :high], dense_ref[i:high, :high])


def near_kernel(low_far_ref, low_near_ref, x_ref, dense_ref, total_ref, o_ref, wide):
    m = x_ref.shape[1]
    half = m // 2
    low_near = low_near_ref[...].astype(F32)
    low_near = jnp.where(on_odd_segment(), low_near, jnp.zeros_like(low_near))
    wide[...] = total_ref[...] + low_near + low_far_ref[...].astype(F32)
    wide[...] += contract(x_ref[...], dense_ref[...])
    for t in range(0, 16, 2):
        parts = []
        for u in (t, t + 1):
            head = wide[12 * u : 12 * u + 8, :]
            left = wide[12 * u + 8 : 12 * u + 12, :half]
            right = wide[12 * u + 8 : 12 * u + 12, half:]
            parts.append(jnp.concatenate([head, jnp.concatenate([left, right], 0)], 1))
        o_ref[8 * t : 8 * t + 16, :] = jnp.concatenate(parts, 0).astype(BF16)


def call(kernel, name, outs, mib, *args, scratch=(), flops=0, far_off=(), far_out=False):
    several = isinstance(outs, tuple)
    size = sum(a.size * a.dtype.itemsize for a in args)
    in_specs = vmem_specs(len(args))
    for k in far_off:
        in_specs[k] = pl.BlockSpec(memory_space=pltpu.HBM)
    out_spec = pl.BlockSpec(memory_space=pltpu.HBM if far_out else pltpu.VMEM)
    return pl.pallas_call(
        kernel,
        out_shape=outs,
        in_specs=in_specs,
        out_specs=tuple(vmem_specs(len(outs))) if several else out_spec,
        scratch_shapes=list(scratch),
        compiler_params=params(mib),
        cost_estimate=pl.CostEstimate(flops=flops, bytes_accessed=size, transcendentals=0),
        name=name,
    )(*args)


def passed_along(shard, by):
    length = lax.axis_size("seg")
    pairs = [(s, s + by) for s in range(length) if 0 <= s + by < length]
    return lax.ppermute(shard, "seg", pairs)


def traded(shard):
    length, places = lax.axis_size("seg"), lax.axis_size("trait")
    pairs = [(s * places + p, (s ^ 1) * places + swapped(p)) for s in range(length) for p in range(places)]
    return lax.ppermute(shard, ("seg", "trait"), pairs)


def exchange(packed):
    rows, lanes = packed.shape
    moved = lax.all_to_all(packed.reshape(16, rows // 16, lanes), "trait", 0, 0, tiled=True)
    return moved.reshape(rows, lanes)


def local(effects, precision, band):
    chains, traits, m = effects.shape
    width = band.shape[1]
    rows = chains * traits
    packed_shape = (8 * chains, m + m // 2)
    struct = jax.ShapeDtypeStruct

    flat = effects.transpose(1, 0, 2).reshape(rows, m)
    packed = call(
        pack_kernel, "pack", struct(packed_shape, BF16), 63, flat,
        far_off=(0,), far_out=True,
        scratch=[
            pltpu.VMEM((rows, m), BF16),
            pltpu.VMEM((m // LANES, rows, LANES), F32),
            pltpu.VMEM(packed_shape, BF16),
            pltpu.SemaphoreType.DMA((4,)),
            pltpu.SemaphoreType.DMA((5,)),
        ],
    )
    square = struct((m, m), BF16)
    within, following, last = call(
        skew_kernel, "skew", (square, square, square), 16, band, flops=m * width
    )
    thin = struct((rows, m), BF16)
    wide = struct((rows, m), F32)
    gathered, following = lax.optimization_barrier((exchange(packed), following))
    mixed = call(mix_kernel, "mix", thin, 16, gathered, precision, flops=4 * rows * rows * m)
    far = passed_along(mixed, -2)
    low_near = call(lower_near_kernel, "lower_near", thin, 16, mixed, following, flops=2 * rows * m * m)
    low_near = traded(low_near)
    low_far = call(lower_far_kernel, "lower_far", wide, 16, mixed, last, flops=rows * m * m)
    low_far = call(join_kernel, "join", thin, 8, low_far, low_near)
    low_far = passed_along(low_far, 2)
    near = traded(call(choose_kernel, "choose", thin, 8, mixed, far))
    total = call(own_kernel, "own", wide, 16, mixed, within, flops=4 * rows * m * m)
    total = call(far_kernel, "far", wide, 16, far, last, total, flops=rows * m * m)
    packed = call(
        near_kernel, "near", struct(packed_shape, BF16), 16, low_far, low_near, near, following, total,
        flops=2 * rows * m * m, scratch=[pltpu.VMEM((rows, m), F32)],
    )
    flat = call(
        unpack_kernel, "unpack", struct((rows, m), BF16), 8, exchange(packed),
        scratch=[pltpu.VMEM((packed_shape[1] // LANES, packed_shape[0], LANES), F32)],
    )
    return flat.reshape(traits, chains, m).transpose(1, 0, 2)


def solution(mesh):
    in_specs = (P(None, "trait", "seg"), P(), P("seg", None))
    out_specs = P(None, "trait", "seg")
    return jax.shard_map(local, mesh=mesh, in_specs=in_specs, out_specs=out_specs, check_vma=False)
```

```python
import jax
import jax.numpy as jnp
from jax import lax
from jax.experimental import pallas as pl
from jax.experimental.pallas import tpu as pltpu
from jax.sharding import PartitionSpec as P

F32 = jnp.float32
BF16 = jnp.bfloat16
LANES = 128
MIB = 1 << 20


def vmem_specs(count):
    return [pl.BlockSpec(memory_space=pltpu.VMEM)] * count


def params(mib):
    return pltpu.CompilerParams(vmem_limit_bytes=mib * MIB)


def swapped(place):
    return 8 * (place % 2) + 2 * (place // 2 % 4) + place // 8


def chain_places():
    odd = lax.rem(lax.axis_index("seg"), 2) == 1
    return [jnp.where(odd, swapped(p), p) for p in range(16)]


def pack_kernel(x_ref, o_ref, near, wide, packed, in_sems, out_sems):
    rows, m = x_ref.shape
    blocks = m // LANES
    chunks = in_sems.shape[0]
    part = m // chunks
    chains = chain_places()
    copies = []
    for q in range(chunks):
        lanes = pl.ds(q * part, part)
        copies.append(pltpu.make_async_copy(x_ref.at[:, lanes], near.at[:, lanes], in_sems.at[q]))
        copies[-1].start()
    out = []

    def send(first, size):
        lanes = pl.ds(first, size)
        out.append(pltpu.make_async_copy(packed.at[:, lanes], o_ref.at[:, lanes], out_sems.at[len(out)]))
        out[-1].start()

    for q in range(chunks):
        copies[q].wait()
        for k in range(q * blocks // chunks, (q + 1) * blocks // chunks):
            wide[k] = near[:, k * LANES : (k + 1) * LANES].astype(F32)
            for p in range(0, 16, 2):
                parts = [wide[k, pl.ds(d, 8, stride=16), :] for d in chains[p : p + 2]]
                packed[8 * p : 8 * p + 16, k * LANES : (k + 1) * LANES] = jnp.concatenate(parts, 0).astype(BF16)
        send(q * part, part)
    for p in range(0, 16, 2):
        for k in range(blocks // 2):
            parts = [
                wide[k + h, pl.ds(128 + d, 4, stride=16), :]
                for d in chains[p : p + 2]
                for h in (0, blocks // 2)
            ]
            packed[8 * p : 8 * p + 16, m + k * LANES : m + (k + 1) * LANES] = jnp.concatenate(parts, 0).astype(BF16)
    send(m, m // 2)
    for copy in out:
        copy.wait()


def unpack_kernel(x_ref, o_ref, wide):
    m = o_ref.shape[1]
    blocks = m // LANES
    chains = chain_places()
    for k in range(wide.shape[0]):
        for p in range(0, 16, 2):
            pair = x_ref[8 * p : 8 * p + 16, k * LANES : (k + 1) * LANES].astype(F32)
            for h in range(2):
                wide[k, pl.ds(pl.multiple_of(8 * chains[p + h], 8), 8), :] = pair[8 * h : 8 * h + 8]
    for k in range(blocks):
        lanes = pl.ds(k * LANES, LANES)
        for j in range(8):
            o_ref[16 * j : 16 * j + 16, lanes] = wide[k, pl.ds(j, 16, stride=8), :].astype(BF16)
        half, place = divmod(k, blocks // 2)
        for j in range(4):
            tail = wide[blocks + place, pl.ds(j + 4 * half, 16, stride=8), :]
            o_ref[128 + 16 * j : 144 + 16 * j, lanes] = tail.astype(BF16)


def mix_kernel(x_ref, p_ref, o_ref):
    m = o_ref.shape[1]
    half = m // 2
    blank = jnp.zeros((4, p_ref.shape[1]), F32)
    heads, lows, highs = [], [], []
    for t in range(16):
        heads.append(p_ref[12 * t : 12 * t + 8, :])
        tail = p_ref[12 * t + 8 : 12 * t + 12, :]
        lows += [tail, blank]
        highs += [blank, tail]
    head = jnp.concatenate(heads, 0)
    for first, tails in ((0, lows), (half, highs)):
        weights = jnp.concatenate([head, jnp.concatenate(tails, 0)], 0).T
        upper = weights.astype(BF16)
        lower = (weights - upper.astype(F32)).astype(BF16)
        values = jnp.concatenate([x_ref[:, first : first + half], x_ref[:, m:]], 0)
        total = jnp.dot(upper, values, preferred_element_type=F32)
        total += jnp.dot(lower, values, preferred_element_type=F32)
        o_ref[:, first : first + half] = total.astype(BF16)

def lower_near_kernel(x_ref, dense_ref, o_ref):
    o_ref[...] = jnp.dot(x_ref[...], dense_ref[...], preferred_element_type=F32).astype(BF16)


def lower_far_kernel(x_ref, dense_ref, o_ref):
    depth = 256
    for i in range(0, x_ref.shape[1], depth):
        part = jnp.dot(x_ref[:, i:], dense_ref[i:, i : i + depth], preferred_element_type=F32)
        o_ref[:, i : i + depth] = part.astype(BF16)


def skew_rows(band_ref, dense_refs, first):
    m, width = band_ref.shape
    rows = pl.ds(first, LANES)

    def put(col, tile):
        if col < m + width:
            dense_refs[col // m][rows, pl.ds(col % m, LANES)] = tile

    a = lax.broadcasted_iota(jnp.int32, (LANES, LANES), 0)
    b = lax.broadcasted_iota(jnp.int32, (LANES, LANES), 1)
    ahead = b > a
    zero = jnp.zeros((LANES, LANES), F32)
    before = zero
    for d in range(width // LANES + 1):
        if d < width // LANES:
            tile = band_ref[rows, d * LANES : (d + 1) * LANES].astype(F32)
            now = pltpu.roll(tile, 1, 1, stride=1, stride_axis=0)
        else:
            now = zero
        put(first + d * LANES, jnp.where(ahead, now, before).astype(BF16))
        before = now
    if first % 256:
        put(first - LANES, zero.astype(BF16))
    else:
        put(first + width + LANES, zero.astype(BF16))


def skew_kernel(band_ref, *dense_refs):
    for first in range(0, band_ref.shape[0], LANES):
        skew_rows(band_ref, dense_refs, first)


def contract(values, dense):
    return lax.dot_general(values, dense, (((1,), (1,)), ((), ())), preferred_element_type=F32)


def own_kernel(x_ref, dense_ref, o_ref):
    m = x_ref.shape[1]
    depth = 256
    for i in range(0, m, depth):
        high = i + depth
        total = x_ref[:, i:high].astype(F32)
        total += jnp.dot(x_ref[:, :high], dense_ref[:high, i:high], preferred_element_type=F32)
        total += contract(x_ref[:, i:], dense_ref[i:high, i:m])
        o_ref[:, i:high] = total


def far_kernel(low_ref, x_ref, dense_ref, total_ref, o_ref):
    m = x_ref.shape[1]
    depth = 256
    for i in range(0, m, depth):
        high = i + depth
        part = total_ref[:, i:high] + low_ref[:, i:high].astype(F32)
        o_ref[:, i:high] = part + contract(x_ref[:, :high], dense_ref[i:high, :high])


def near_kernel(x_ref, dense_ref, total_ref, o_ref):
    o_ref[...] = total_ref[...] + contract(x_ref[...], dense_ref[...])


def finish_kernel(total_ref, far_ref, o_ref, wide):
    m = total_ref.shape[1]
    half = m // 2
    wide[...] = total_ref[...] + far_ref[...].astype(F32)
    for t in range(0, 16, 2):
        parts = []
        for u in (t, t + 1):
            head = wide[12 * u : 12 * u + 8, :]
            left = wide[12 * u + 8 : 12 * u + 12, :half]
            right = wide[12 * u + 8 : 12 * u + 12, half:]
            parts.append(jnp.concatenate([head, jnp.concatenate([left, right], 0)], 1))
        o_ref[8 * t : 8 * t + 16, :] = jnp.concatenate(parts, 0).astype(BF16)


def call(kernel, name, outs, mib, *args, scratch=(), flops=0, far_off=(), far_out=False):
    several = isinstance(outs, tuple)
    size = sum(a.size * a.dtype.itemsize for a in args)
    in_specs = vmem_specs(len(args))
    for k in far_off:
        in_specs[k] = pl.BlockSpec(memory_space=pltpu.HBM)
    out_spec = pl.BlockSpec(memory_space=pltpu.HBM if far_out else pltpu.VMEM)
    return pl.pallas_call(
        kernel,
        out_shape=outs,
        in_specs=in_specs,
        out_specs=tuple(vmem_specs(len(outs))) if several else out_spec,
        scratch_shapes=list(scratch),
        compiler_params=params(mib),
        cost_estimate=pl.CostEstimate(flops=flops, bytes_accessed=size, transcendentals=0),
        name=name,
    )(*args)


def passed_along(shard, by):
    length, places = lax.axis_size("seg"), lax.axis_size("trait")
    pairs = []
    for s in range(length):
        for p in range(places):
            if 0 <= s + by < length:
                pairs.append((s * places + p, (s + by) * places + (swapped(p) if by % 2 else p)))
    return lax.ppermute(shard, ("seg", "trait"), pairs)


def exchange(packed):
    rows, lanes = packed.shape
    moved = lax.all_to_all(packed.reshape(16, rows // 16, lanes), "trait", 0, 0, tiled=True)
    return moved.reshape(rows, lanes)


def local(effects, precision, band):
    chains, traits, m = effects.shape
    width = band.shape[1]
    rows = chains * traits
    packed_shape = (8 * chains, m + m // 2)
    struct = jax.ShapeDtypeStruct

    flat = effects.transpose(1, 0, 2).reshape(rows, m)
    packed = call(
        pack_kernel, "pack", struct(packed_shape, BF16), 63, flat,
        far_off=(0,), far_out=True,
        scratch=[
            pltpu.VMEM((rows, m), BF16),
            pltpu.VMEM((m // LANES, rows, LANES), F32),
            pltpu.VMEM(packed_shape, BF16),
            pltpu.SemaphoreType.DMA((4,)),
            pltpu.SemaphoreType.DMA((5,)),
        ],
    )
    square = struct((m, m), BF16)
    within, following, last = call(
        skew_kernel, "skew", (square, square, square), 16, band, flops=m * width
    )
    thin = struct((rows, m), BF16)
    wide = struct((rows, m), F32)
    gathered, following = lax.optimization_barrier((exchange(packed), following))
    mixed = call(mix_kernel, "mix", thin, 16, gathered, precision, flops=4 * rows * rows * m)
    near = passed_along(mixed, -1)
    low_near = call(lower_near_kernel, "lower_near", thin, 16, mixed, following, flops=2 * rows * m * m)
    later, low_near = lax.optimization_barrier((mixed, low_near))
    low_near = passed_along(low_near, 1)
    far = passed_along(later, -2)
    low_far = call(lower_far_kernel, "lower_far", thin, 16, mixed, last, flops=rows * m * m)
    low_far = passed_along(low_far, 2)
    total = call(own_kernel, "own", wide, 16, mixed, within, flops=4 * rows * m * m)
    total = call(near_kernel, "near", wide, 16, near, following, total, flops=2 * rows * m * m)
    total = call(far_kernel, "far", wide, 16, low_near, far, last, total, flops=rows * m * m)
    packed = call(
        finish_kernel, "finish", struct(packed_shape, BF16), 16, total, low_far,
        scratch=[pltpu.VMEM((rows, m), F32)],
    )
    flat = call(
        unpack_kernel, "unpack", struct((rows, m), BF16), 8, exchange(packed),
        scratch=[pltpu.VMEM((packed_shape[1] // LANES, packed_shape[0], LANES), F32)],
    )
    return flat.reshape(traits, chains, m).transpose(1, 0, 2)


def solution(mesh):
    in_specs = (P(None, "trait", "seg"), P(), P("seg", None))
    out_specs = P(None, "trait", "seg")
    return jax.shard_map(local, mesh=mesh, in_specs=in_specs, out_specs=out_specs, check_vma=False)
```

```python
import jax
import jax.numpy as jnp
from jax import lax
from jax.experimental import pallas as pl
from jax.experimental.pallas import tpu as pltpu
from jax.sharding import PartitionSpec as P

F32 = jnp.float32
BF16 = jnp.bfloat16
LANES = 128
MIB = 1 << 20


def vmem_specs(count):
    return [pl.BlockSpec(memory_space=pltpu.VMEM)] * count


def params(mib):
    return pltpu.CompilerParams(vmem_limit_bytes=mib * MIB)


def swapped(place):
    return 8 * (place % 2) + 2 * (place // 2 % 4) + place // 8


def chain_places():
    odd = lax.rem(lax.axis_index("seg"), 2) == 1
    return [jnp.where(odd, swapped(p), p) for p in range(16)]


def pack_kernel(x_ref, o_ref, near, wide, packed, in_sems, out_sems):
    rows, m = x_ref.shape
    blocks = m // LANES
    chunks = in_sems.shape[0]
    part = m // chunks
    chains = chain_places()
    copies = []
    for q in range(chunks):
        lanes = pl.ds(q * part, part)
        copies.append(pltpu.make_async_copy(x_ref.at[:, lanes], near.at[:, lanes], in_sems.at[q]))
        copies[-1].start()
    out = []

    def send(first, size):
        lanes = pl.ds(first, size)
        out.append(pltpu.make_async_copy(packed.at[:, lanes], o_ref.at[:, lanes], out_sems.at[len(out)]))
        out[-1].start()

    for q in range(chunks):
        copies[q].wait()
        for k in range(q * blocks // chunks, (q + 1) * blocks // chunks):
            wide[k] = near[:, k * LANES : (k + 1) * LANES].astype(F32)
            for p in range(0, 16, 2):
                parts = [wide[k, pl.ds(d, 8, stride=16), :] for d in chains[p : p + 2]]
                packed[8 * p : 8 * p + 16, k * LANES : (k + 1) * LANES] = jnp.concatenate(parts, 0).astype(BF16)
        send(q * part, part)
    for p in range(0, 16, 2):
        for k in range(blocks // 2):
            parts = [
                wide[k + h, pl.ds(128 + d, 4, stride=16), :]
                for d in chains[p : p + 2]
                for h in (0, blocks // 2)
            ]
            packed[8 * p : 8 * p + 16, m + k * LANES : m + (k + 1) * LANES] = jnp.concatenate(parts, 0).astype(BF16)
    send(m, m // 2)
    for copy in out:
        copy.wait()


def unpack_kernel(x_ref, o_ref, wide):
    m = o_ref.shape[1]
    blocks = m // LANES
    chains = chain_places()
    for k in range(wide.shape[0]):
        for p in range(0, 16, 2):
            pair = x_ref[8 * p : 8 * p + 16, k * LANES : (k + 1) * LANES].astype(F32)
            for h in range(2):
                wide[k, pl.ds(pl.multiple_of(8 * chains[p + h], 8), 8), :] = pair[8 * h : 8 * h + 8]
    for k in range(blocks):
        lanes = pl.ds(k * LANES, LANES)
        for j in range(8):
            o_ref[16 * j : 16 * j + 16, lanes] = wide[k, pl.ds(j, 16, stride=8), :].astype(BF16)
        half, place = divmod(k, blocks // 2)
        for j in range(4):
            tail = wide[blocks + place, pl.ds(j + 4 * half, 16, stride=8), :]
            o_ref[128 + 16 * j : 144 + 16 * j, lanes] = tail.astype(BF16)


def mix_kernel(x_ref, p_ref, o_ref):
    m = o_ref.shape[1]
    half = m // 2
    blank = jnp.zeros((4, p_ref.shape[1]), F32)
    heads, lows, highs = [], [], []
    for t in range(16):
        heads.append(p_ref[12 * t : 12 * t + 8, :])
        tail = p_ref[12 * t + 8 : 12 * t + 12, :]
        lows += [tail, blank]
        highs += [blank, tail]
    head = jnp.concatenate(heads, 0)
    for first, tails in ((0, lows), (half, highs)):
        weights = jnp.concatenate([head, jnp.concatenate(tails, 0)], 0).T
        upper = weights.astype(BF16)
        lower = (weights - upper.astype(F32)).astype(BF16)
        values = jnp.concatenate([x_ref[:, first : first + half], x_ref[:, m:]], 0)
        total = jnp.dot(upper, values, preferred_element_type=F32)
        total += jnp.dot(lower, values, preferred_element_type=F32)
        o_ref[:, first : first + half] = total.astype(BF16)

def lower_near_kernel(x_ref, dense_ref, o_ref):
    o_ref[...] = jnp.dot(x_ref[...], dense_ref[...], preferred_element_type=F32).astype(BF16)


def lower_far_kernel(x_ref, dense_ref, o_ref):
    depth = 256
    for i in range(0, x_ref.shape[1], depth):
        part = jnp.dot(x_ref[:, i:], dense_ref[i:, i : i + depth], preferred_element_type=F32)
        o_ref[:, i : i + depth] = part.astype(BF16)


def skew_rows(band_ref, dense_refs, first):
    m, width = band_ref.shape
    rows = pl.ds(first, LANES)

    def put(col, tile):
        if col < m + width:
            dense_refs[col // m][rows, pl.ds(col % m, LANES)] = tile

    a = lax.broadcasted_iota(jnp.int32, (LANES, LANES), 0)
    b = lax.broadcasted_iota(jnp.int32, (LANES, LANES), 1)
    ahead = b > a
    zero = jnp.zeros((LANES, LANES), F32)
    before = zero
    for d in range(width // LANES + 1):
        if d < width // LANES:
            tile = band_ref[rows, d * LANES : (d + 1) * LANES].astype(F32)
            now = pltpu.roll(tile, 1, 1, stride=1, stride_axis=0)
        else:
            now = zero
        put(first + d * LANES, jnp.where(ahead, now, before).astype(BF16))
        before = now
    if first % 256:
        put(first - LANES, zero.astype(BF16))
    else:
        put(first + width + LANES, zero.astype(BF16))


def skew_kernel(band_ref, *dense_refs):
    for first in range(0, band_ref.shape[0], LANES):
        skew_rows(band_ref, dense_refs, first)


def contract(values, dense):
    return lax.dot_general(values, dense, (((1,), (1,)), ((), ())), preferred_element_type=F32)


def own_kernel(x_ref, dense_ref, o_ref):
    m = x_ref.shape[1]
    depth = 256
    for i in range(0, m, depth):
        high = i + depth
        total = x_ref[:, i:high].astype(F32)
        total += jnp.dot(x_ref[:, :high], dense_ref[:high, i:high], preferred_element_type=F32)
        total += contract(x_ref[:, i:], dense_ref[i:high, i:m])
        o_ref[:, i:high] = total


def far_kernel(low_ref, x_ref, dense_ref, total_ref, o_ref):
    m = x_ref.shape[1]
    depth = 256
    for i in range(0, m, depth):
        high = i + depth
        part = total_ref[:, i:high] + low_ref[:, i:high].astype(F32)
        o_ref[:, i:high] = part + contract(x_ref[:, :high], dense_ref[i:high, :high])


def near_kernel(cross_ref, pair_ref, dense_ref, total_ref, o_ref):
    x = (cross_ref[...].astype(F32) + pair_ref[...].astype(F32)).astype(BF16)
    o_ref[...] = total_ref[...] + contract(x, dense_ref[...])


def finish_kernel(far_ref, pair_ref, total_ref, o_ref, wide):
    m = total_ref.shape[1]
    half = m // 2
    wide[...] = total_ref[...] + far_ref[...].astype(F32) + pair_ref[...].astype(F32)
    for t in range(0, 16, 2):
        parts = []
        for u in (t, t + 1):
            head = wide[12 * u : 12 * u + 8, :]
            left = wide[12 * u + 8 : 12 * u + 12, :half]
            right = wide[12 * u + 8 : 12 * u + 12, half:]
            parts.append(jnp.concatenate([head, jnp.concatenate([left, right], 0)], 1))
        o_ref[8 * t : 8 * t + 16, :] = jnp.concatenate(parts, 0).astype(BF16)


def call(kernel, name, outs, mib, *args, scratch=(), flops=0, far_off=(), far_out=False):
    several = isinstance(outs, tuple)
    size = sum(a.size * a.dtype.itemsize for a in args)
    in_specs = vmem_specs(len(args))
    for k in far_off:
        in_specs[k] = pl.BlockSpec(memory_space=pltpu.HBM)
    out_spec = pl.BlockSpec(memory_space=pltpu.HBM if far_out else pltpu.VMEM)
    return pl.pallas_call(
        kernel,
        out_shape=outs,
        in_specs=in_specs,
        out_specs=tuple(vmem_specs(len(outs))) if several else out_spec,
        scratch_shapes=list(scratch),
        compiler_params=params(mib),
        cost_estimate=pl.CostEstimate(flops=flops, bytes_accessed=size, transcendentals=0),
        name=name,
    )(*args)


def passed_along(shard, by, sources):
    length, places = lax.axis_size("seg"), lax.axis_size("trait")
    pairs = []
    for s in sources:
        for p in range(places):
            if 0 <= s + by < length:
                pairs.append((s * places + p, (s + by) * places + (swapped(p) if by % 2 else p)))
    return lax.ppermute(shard, ("seg", "trait"), pairs)


def exchange(packed):
    rows, lanes = packed.shape
    moved = lax.all_to_all(packed.reshape(16, rows // 16, lanes), "trait", 0, 0, tiled=True)
    return moved.reshape(rows, lanes)


def local(effects, precision, band):
    chains, traits, m = effects.shape
    width = band.shape[1]
    rows = chains * traits
    packed_shape = (8 * chains, m + m // 2)
    struct = jax.ShapeDtypeStruct

    flat = effects.transpose(1, 0, 2).reshape(rows, m)
    packed = call(
        pack_kernel, "pack", struct(packed_shape, BF16), 63, flat,
        far_off=(0,), far_out=True,
        scratch=[
            pltpu.VMEM((rows, m), BF16),
            pltpu.VMEM((m // LANES, rows, LANES), F32),
            pltpu.VMEM(packed_shape, BF16),
            pltpu.SemaphoreType.DMA((4,)),
            pltpu.SemaphoreType.DMA((5,)),
        ],
    )
    square = struct((m, m), BF16)
    within, following, last = call(
        skew_kernel, "skew", (square, square, square), 16, band, flops=m * width
    )
    thin = struct((rows, m), BF16)
    wide = struct((rows, m), F32)
    gathered, following = lax.optimization_barrier((exchange(packed), following))
    mixed = call(mix_kernel, "mix", thin, 16, gathered, precision, flops=4 * rows * rows * m)
    every = range(lax.axis_size("seg"))
    even, odd = every[::2], every[1::2]
    cross = passed_along(mixed, -1, even)
    low_near = call(lower_near_kernel, "lower_near", thin, 16, mixed, following, flops=2 * rows * m * m)
    low_cross = passed_along(low_near, 1, odd)
    later, after = lax.optimization_barrier((mixed, low_near))
    far = passed_along(later, -2, every)
    low_far = call(lower_far_kernel, "lower_far", thin, 16, later, last, flops=rows * m * m)
    later, after, low_far = lax.optimization_barrier((later, after, low_far))
    low_far = passed_along(low_far, 2, every)
    pair = passed_along(later, -1, odd)
    low_pair = passed_along(after, 1, even)
    total = call(own_kernel, "own", wide, 16, mixed, within, flops=4 * rows * m * m)
    total = call(far_kernel, "far", wide, 16, low_cross, far, last, total, flops=rows * m * m)
    total = call(near_kernel, "near", wide, 16, cross, pair, following, total, flops=2 * rows * m * m)
    packed = call(
        finish_kernel, "finish", struct(packed_shape, BF16), 16, low_far, low_pair, total,
        scratch=[pltpu.VMEM((rows, m), F32)],
    )
    flat = call(
        unpack_kernel, "unpack", struct((rows, m), BF16), 8, exchange(packed),
        scratch=[pltpu.VMEM((packed_shape[1] // LANES, packed_shape[0], LANES), F32)],
    )
    return flat.reshape(traits, chains, m).transpose(1, 0, 2)


def solution(mesh):
    in_specs = (P(None, "trait", "seg"), P(), P("seg", None))
    out_specs = P(None, "trait", "seg")
    return jax.shard_map(local, mesh=mesh, in_specs=in_specs, out_specs=out_specs, check_vma=False)
```

```python
import jax
import jax.numpy as jnp
from jax import lax
from jax.experimental import pallas as pl
from jax.experimental.pallas import tpu as pltpu
from jax.sharding import PartitionSpec as P

F32 = jnp.float32
BF16 = jnp.bfloat16
LANES = 128
MIB = 1 << 20


def vmem_specs(count):
    return [pl.BlockSpec(memory_space=pltpu.VMEM)] * count


def params(mib):
    return pltpu.CompilerParams(vmem_limit_bytes=mib * MIB)


def swapped(place):
    return 8 * (place % 2) + 2 * (place // 2 % 4) + place // 8


def chain_places():
    odd = lax.rem(lax.axis_index("seg"), 2) == 1
    return [jnp.where(odd, swapped(p), p) for p in range(16)]


def pack_kernel(x_ref, o_ref, near, wide, packed, in_sems, out_sems):
    rows, m = x_ref.shape
    blocks = m // LANES
    chunks = in_sems.shape[0]
    part = m // chunks
    chains = chain_places()
    copies = []
    for q in range(chunks):
        lanes = pl.ds(q * part, part)
        copies.append(pltpu.make_async_copy(x_ref.at[:, lanes], near.at[:, lanes], in_sems.at[q]))
        copies[-1].start()
    out = []

    def send(first, size):
        lanes = pl.ds(first, size)
        out.append(pltpu.make_async_copy(packed.at[:, lanes], o_ref.at[:, lanes], out_sems.at[len(out)]))
        out[-1].start()

    for q in range(chunks):
        copies[q].wait()
        for k in range(q * blocks // chunks, (q + 1) * blocks // chunks):
            wide[k] = near[:, k * LANES : (k + 1) * LANES].astype(F32)
            for p in range(0, 16, 2):
                parts = [wide[k, pl.ds(d, 8, stride=16), :] for d in chains[p : p + 2]]
                packed[8 * p : 8 * p + 16, k * LANES : (k + 1) * LANES] = jnp.concatenate(parts, 0).astype(BF16)
        send(q * part, part)
    for p in range(0, 16, 2):
        for k in range(blocks // 2):
            parts = [
                wide[k + h, pl.ds(128 + d, 4, stride=16), :]
                for d in chains[p : p + 2]
                for h in (0, blocks // 2)
            ]
            packed[8 * p : 8 * p + 16, m + k * LANES : m + (k + 1) * LANES] = jnp.concatenate(parts, 0).astype(BF16)
    send(m, m // 2)
    for copy in out:
        copy.wait()


def unpack_kernel(x_ref, o_ref, wide, held, sems):
    m = o_ref.shape[1]
    blocks = m // LANES
    chunks = sems.shape[0]
    chains = chain_places()

    def widen(k):
        for p in range(0, 16, 2):
            pair = x_ref[8 * p : 8 * p + 16, k * LANES : (k + 1) * LANES].astype(F32)
            for h in range(2):
                wide[k, pl.ds(pl.multiple_of(8 * chains[p + h], 8), 8), :] = pair[8 * h : 8 * h + 8]

    for k in range(blocks, wide.shape[0]):
        widen(k)
    copies = []
    for q in range(chunks):
        for k in range(q * blocks // chunks, (q + 1) * blocks // chunks):
            widen(k)
            lanes = pl.ds(k * LANES, LANES)
            for j in range(8):
                held[16 * j : 16 * j + 16, lanes] = wide[k, pl.ds(j, 16, stride=8), :].astype(BF16)
            half, place = divmod(k, blocks // 2)
            for j in range(4):
                tail = wide[blocks + place, pl.ds(j + 4 * half, 16, stride=8), :]
                held[128 + 16 * j : 144 + 16 * j, lanes] = tail.astype(BF16)
        lanes = pl.ds(q * (m // chunks), m // chunks)
        copies.append(pltpu.make_async_copy(held.at[:, lanes], o_ref.at[:, lanes], sems.at[q]))
        copies[-1].start()
    for copy in copies:
        copy.wait()


def mix_kernel(x_ref, p_ref, o_ref):
    m = o_ref.shape[1]
    half = m // 2
    blank = jnp.zeros((4, p_ref.shape[1]), F32)
    heads, lows, highs = [], [], []
    for t in range(16):
        heads.append(p_ref[12 * t : 12 * t + 8, :])
        tail = p_ref[12 * t + 8 : 12 * t + 12, :]
        lows += [tail, blank]
        highs += [blank, tail]
    head = jnp.concatenate(heads, 0)
    for first, tails in ((0, lows), (half, highs)):
        weights = jnp.concatenate([head, jnp.concatenate(tails, 0)], 0).T
        upper = weights.astype(BF16)
        lower = (weights - upper.astype(F32)).astype(BF16)
        values = jnp.concatenate([x_ref[:, first : first + half], x_ref[:, m:]], 0)
        total = jnp.dot(upper, values, preferred_element_type=F32)
        total += jnp.dot(lower, values, preferred_element_type=F32)
        o_ref[:, first : first + half] = total.astype(BF16)

def lower_near_kernel(x_ref, dense_ref, o_ref):
    o_ref[...] = jnp.dot(x_ref[...], dense_ref[...], preferred_element_type=F32).astype(BF16)


def lower_far_kernel(x_ref, dense_ref, o_ref):
    depth = 256
    for i in range(0, x_ref.shape[1], depth):
        part = jnp.dot(x_ref[:, i:], dense_ref[i:, i : i + depth], preferred_element_type=F32)
        o_ref[:, i : i + depth] = part.astype(BF16)


def skew_rows(band_ref, dense_refs, first):
    m, width = band_ref.shape
    rows = pl.ds(first, LANES)

    def put(col, tile):
        if col < m + width:
            dense_refs[col // m][rows, pl.ds(col % m, LANES)] = tile

    a = lax.broadcasted_iota(jnp.int32, (LANES, LANES), 0)
    b = lax.broadcasted_iota(jnp.int32, (LANES, LANES), 1)
    ahead = b > a
    zero = jnp.zeros((LANES, LANES), F32)
    before = zero
    for d in range(width // LANES + 1):
        if d < width // LANES:
            tile = band_ref[rows, d * LANES : (d + 1) * LANES].astype(F32)
            now = pltpu.roll(tile, 1, 1, stride=1, stride_axis=0)
        else:
            now = zero
        put(first + d * LANES, jnp.where(ahead, now, before).astype(BF16))
        before = now
    if first % 256:
        put(first - LANES, zero.astype(BF16))
    else:
        put(first + width + LANES, zero.astype(BF16))


def skew_kernel(band_ref, *dense_refs):
    for first in range(0, band_ref.shape[0], LANES):
        skew_rows(band_ref, dense_refs, first)


def contract(values, dense):
    return lax.dot_general(values, dense, (((1,), (1,)), ((), ())), preferred_element_type=F32)


def own_kernel(x_ref, dense_ref, o_ref):
    m = x_ref.shape[1]
    depth = 256
    for i in range(0, m, depth):
        high = i + depth
        total = x_ref[:, i:high].astype(F32)
        total += jnp.dot(x_ref[:, :high], dense_ref[:high, i:high], preferred_element_type=F32)
        total += contract(x_ref[:, i:], dense_ref[i:high, i:m])
        o_ref[:, i:high] = total


def far_kernel(x_ref, dense_ref, total_ref, o_ref):
    m = x_ref.shape[1]
    depth = 256
    for i in range(0, m, depth):
        high = i + depth
        o_ref[:, i:high] = total_ref[:, i:high] + contract(x_ref[:, :high], dense_ref[i:high, :high])


def on_odd_segment():
    return lax.rem(lax.axis_index("seg"), 2) == 1


def choose_kernel(own_ref, far_ref, o_ref):
    @pl.when(on_odd_segment())
    def _():
        o_ref[...] = own_ref[...]

    @pl.when(jnp.logical_not(on_odd_segment()))
    def _():
        o_ref[...] = far_ref[...]


def near_kernel(x_ref, low_near_ref, low_far_ref, dense_ref, total_ref, o_ref, wide):
    m = x_ref.shape[1]
    half = m // 2
    depth = 256
    for i in range(0, m, depth):
        lanes = pl.ds(i, depth)
        total = total_ref[:, lanes] + low_near_ref[:, lanes].astype(F32) + low_far_ref[:, lanes].astype(F32)
        wide[:, lanes] = total + contract(x_ref[...], dense_ref[lanes, :])
        for t in range(0, 16, 2):
            parts = [wide[12 * u : 12 * u + 8, lanes] for u in (t, t + 1)]
            o_ref[8 * t : 8 * t + 16, lanes] = jnp.concatenate(parts, 0).astype(BF16)
        if i >= half:
            for t in range(0, 16, 2):
                parts = [
                    wide[12 * u + 8 : 12 * u + 12, pl.ds(k, depth)] for u in (t, t + 1) for k in (i - half, i)
                ]
                o_ref[8 * t : 8 * t + 16, pl.ds(half + i, depth)] = jnp.concatenate(parts, 0).astype(BF16)


def call(kernel, name, outs, mib, *args, scratch=(), flops=0, far_off=(), far_out=False):
    several = isinstance(outs, tuple)
    size = sum(a.size * a.dtype.itemsize for a in args)
    in_specs = vmem_specs(len(args))
    for k in far_off:
        in_specs[k] = pl.BlockSpec(memory_space=pltpu.HBM)
    out_spec = pl.BlockSpec(memory_space=pltpu.HBM if far_out else pltpu.VMEM)
    return pl.pallas_call(
        kernel,
        out_shape=outs,
        in_specs=in_specs,
        out_specs=tuple(vmem_specs(len(outs))) if several else out_spec,
        scratch_shapes=list(scratch),
        compiler_params=params(mib),
        cost_estimate=pl.CostEstimate(flops=flops, bytes_accessed=size, transcendentals=0),
        name=name,
    )(*args)


def passed_along(shard, by):
    length, places = lax.axis_size("seg"), lax.axis_size("trait")
    pairs = []
    for s in range(length):
        for p in range(places):
            if 0 <= s + by < length:
                pairs.append((s * places + p, (s + by) * places + (swapped(p) if by % 2 else p)))
    return lax.ppermute(shard, ("seg", "trait"), pairs)


def traded(shard):
    length, places = lax.axis_size("seg"), lax.axis_size("trait")
    pairs = [(s * places + p, (s ^ 1) * places + swapped(p)) for s in range(length) for p in range(places)]
    return lax.ppermute(shard, ("seg", "trait"), pairs)


def exchange(packed):
    rows, lanes = packed.shape
    moved = lax.all_to_all(packed.reshape(16, rows // 16, lanes), "trait", 0, 0, tiled=True)
    return moved.reshape(rows, lanes)


def local(effects, precision, band):
    chains, traits, m = effects.shape
    width = band.shape[1]
    rows = chains * traits
    packed_shape = (8 * chains, m + m // 2)
    struct = jax.ShapeDtypeStruct

    flat = effects.transpose(1, 0, 2).reshape(rows, m)
    packed = call(
        pack_kernel, "pack", struct(packed_shape, BF16), 63, flat,
        far_off=(0,), far_out=True,
        scratch=[
            pltpu.VMEM((rows, m), BF16),
            pltpu.VMEM((m // LANES, rows, LANES), F32),
            pltpu.VMEM(packed_shape, BF16),
            pltpu.SemaphoreType.DMA((4,)),
            pltpu.SemaphoreType.DMA((5,)),
        ],
    )
    square = struct((m, m), BF16)
    within, following, last = call(
        skew_kernel, "skew", (square, square, square), 16, band, flops=m * width
    )
    thin = struct((rows, m), BF16)
    gathered, following = lax.optimization_barrier((exchange(packed), following))
    mixed = call(mix_kernel, "mix", thin, 16, gathered, precision, flops=4 * rows * rows * m)
    far = passed_along(mixed, -2)
    low_near = call(lower_near_kernel, "lower_near", thin, 16, mixed, following, flops=2 * rows * m * m)
    low_near = passed_along(low_near, 1)
    low_far = call(lower_far_kernel, "lower_far", thin, 16, mixed, last, flops=rows * m * m)
    low_far = passed_along(low_far, 2)
    near = traded(call(choose_kernel, "choose", thin, 8, mixed, far))
    wide = struct((rows, m), F32)
    total = call(own_kernel, "own", wide, 16, mixed, within, flops=4 * rows * m * m)
    total = call(far_kernel, "far", wide, 16, far, last, total, flops=rows * m * m)
    packed = call(
        near_kernel, "near", struct(packed_shape, BF16), 16, near, low_near, low_far, following, total,
        flops=2 * rows * m * m, scratch=[pltpu.VMEM((rows, m), F32)],
    )
    flat = call(
        unpack_kernel, "unpack", thin, 8, exchange(packed), far_out=True,
        scratch=[
            pltpu.VMEM((packed_shape[1] // LANES, packed_shape[0], LANES), F32),
            pltpu.VMEM((rows, m), BF16),
            pltpu.SemaphoreType.DMA((4,)),
        ],
    )
    return flat.reshape(traits, chains, m).transpose(1, 0, 2)


def solution(mesh):
    in_specs = (P(None, "trait", "seg"), P(), P("seg", None))
    out_specs = P(None, "trait", "seg")
    return jax.shard_map(local, mesh=mesh, in_specs=in_specs, out_specs=out_specs, check_vma=False)
```

```python
import jax
import jax.numpy as jnp
from jax import lax
from jax.experimental import pallas as pl
from jax.experimental.pallas import tpu as pltpu
from jax.sharding import PartitionSpec as P

F32 = jnp.float32
BF16 = jnp.bfloat16
LANES = 128
MIB = 1 << 20


def vmem_specs(count):
    return [pl.BlockSpec(memory_space=pltpu.VMEM)] * count


def params(mib):
    return pltpu.CompilerParams(vmem_limit_bytes=mib * MIB)


def swapped(place):
    return 8 * (place % 2) + 2 * (place // 2 % 4) + place // 8


def chain_places():
    odd = lax.rem(lax.axis_index("seg"), 2) == 1
    return [jnp.where(odd, swapped(p), p) for p in range(16)]


def pack_kernel(x_ref, o_ref, near, wide, packed, in_sems, out_sems):
    rows, m = x_ref.shape
    blocks = m // LANES
    chunks = in_sems.shape[0]
    part = rows // chunks
    chains = chain_places()
    copies = []
    for q in range(chunks):
        some = pl.ds(q * part, part)
        copies.append(pltpu.make_async_copy(x_ref.at[some], near.at[some], in_sems.at[q]))
        copies[-1].start()
    for q in range(chunks):
        copies[q].wait()
        for k in range(blocks):
            some = pl.ds(q * part, part)
            wide[k, some, :] = near[some, k * LANES : (k + 1) * LANES].astype(F32)
    out = []
    for q, p in enumerate(range(0, 16, 2)):
        some = pl.ds(8 * p, 16)
        for k in range(blocks):
            parts = [wide[k, pl.ds(d, 8, stride=16), :] for d in chains[p : p + 2]]
            packed[some, k * LANES : (k + 1) * LANES] = jnp.concatenate(parts, 0).astype(BF16)
        for k in range(blocks // 2):
            parts = [
                wide[k + h, pl.ds(128 + d, 4, stride=16), :]
                for d in chains[p : p + 2]
                for h in (0, blocks // 2)
            ]
            packed[some, m + k * LANES : m + (k + 1) * LANES] = jnp.concatenate(parts, 0).astype(BF16)
        out.append(pltpu.make_async_copy(packed.at[some], o_ref.at[some], out_sems.at[q]))
        out[-1].start()
    for copy in out:
        copy.wait()


def unpack_kernel(x_ref, o_ref, wide, held, sems):
    m = o_ref.shape[1]
    blocks = m // LANES
    chunks = sems.shape[0]
    chains = chain_places()

    def widen(k):
        for p in range(0, 16, 2):
            pair = x_ref[8 * p : 8 * p + 16, k * LANES : (k + 1) * LANES].astype(F32)
            for h in range(2):
                wide[k, pl.ds(pl.multiple_of(8 * chains[p + h], 8), 8), :] = pair[8 * h : 8 * h + 8]

    for k in range(blocks, wide.shape[0]):
        widen(k)
    copies = []
    for q in range(chunks):
        for k in range(q * blocks // chunks, (q + 1) * blocks // chunks):
            widen(k)
            lanes = pl.ds(k * LANES, LANES)
            for j in range(8):
                held[16 * j : 16 * j + 16, lanes] = wide[k, pl.ds(j, 16, stride=8), :].astype(BF16)
            half, place = divmod(k, blocks // 2)
            for j in range(4):
                tail = wide[blocks + place, pl.ds(j + 4 * half, 16, stride=8), :]
                held[128 + 16 * j : 144 + 16 * j, lanes] = tail.astype(BF16)
        lanes = pl.ds(q * (m // chunks), m // chunks)
        copies.append(pltpu.make_async_copy(held.at[:, lanes], o_ref.at[:, lanes], sems.at[q]))
        copies[-1].start()
    for copy in copies:
        copy.wait()


def weights_kernel(p_ref, upper_ref, lower_ref):
    blank = jnp.zeros((4, p_ref.shape[1]), F32)
    heads, lows, highs = [], [], []
    for t in range(16):
        heads.append(p_ref[12 * t : 12 * t + 8, :])
        tail = p_ref[12 * t + 8 : 12 * t + 12, :]
        lows += [tail, blank]
        highs += [blank, tail]
    head = jnp.concatenate(heads, 0)
    for k, tails in enumerate((lows, highs)):
        weights = jnp.concatenate([head, jnp.concatenate(tails, 0)], 0).T
        upper = weights.astype(BF16)
        upper_ref[k] = upper
        lower_ref[k] = (weights - upper.astype(F32)).astype(BF16)


def mix_kernel(x_ref, upper_ref, lower_ref, o_ref):
    m = o_ref.shape[1]
    half = m // 2
    for k, first in enumerate((0, half)):
        values = jnp.concatenate([x_ref[:, first : first + half], x_ref[:, m:]], 0)
        total = jnp.dot(upper_ref[k], values, preferred_element_type=F32)
        total += jnp.dot(lower_ref[k], values, preferred_element_type=F32)
        o_ref[:, first : first + half] = total.astype(BF16)


def lower_near_kernel(x_ref, dense_ref, o_ref):
    o_ref[...] = jnp.dot(x_ref[...], dense_ref[...], preferred_element_type=F32).astype(BF16)


def lower_far_kernel(x_ref, dense_ref, o_ref):
    depth = 256
    for i in range(0, x_ref.shape[1], depth):
        part = jnp.dot(x_ref[:, i:], dense_ref[i:, i : i + depth], preferred_element_type=F32)
        o_ref[:, i : i + depth] = part.astype(BF16)


def skew_rows(band_ref, dense_refs, first):
    m, width = band_ref.shape
    rows = pl.ds(first, LANES)

    def put(col, tile):
        if col < m + width:
            dense_refs[col // m][rows, pl.ds(col % m, LANES)] = tile

    a = lax.broadcasted_iota(jnp.int32, (LANES, LANES), 0)
    b = lax.broadcasted_iota(jnp.int32, (LANES, LANES), 1)
    ahead = b > a
    zero = jnp.zeros((LANES, LANES), F32)
    before = zero
    for d in range(width // LANES + 1):
        if d < width // LANES:
            tile = band_ref[rows, d * LANES : (d + 1) * LANES].astype(F32)
            now = pltpu.roll(tile, 1, 1, stride=1, stride_axis=0)
        else:
            now = zero
        put(first + d * LANES, jnp.where(ahead, now, before).astype(BF16))
        before = now
    if first % 256:
        put(first - LANES, zero.astype(BF16))
    else:
        put(first + width + LANES, zero.astype(BF16))


def skew_kernel(band_ref, *dense_refs):
    for first in range(0, band_ref.shape[0], LANES):
        skew_rows(band_ref, dense_refs, first)


def contract(values, dense):
    return lax.dot_general(values, dense, (((1,), (1,)), ((), ())), preferred_element_type=F32)


def own_kernel(x_ref, dense_ref, o_ref):
    m = x_ref.shape[1]
    depth = 256
    for i in range(0, m, depth):
        high = i + depth
        total = x_ref[:, i:high].astype(F32)
        total += jnp.dot(x_ref[:, :high], dense_ref[:high, i:high], preferred_element_type=F32)
        total += contract(x_ref[:, i:], dense_ref[i:high, i:m])
        o_ref[:, i:high] = total


def far_kernel(x_ref, dense_ref, total_ref, o_ref):
    m = x_ref.shape[1]
    depth = 256
    for i in range(0, m, depth):
        high = i + depth
        o_ref[:, i:high] = total_ref[:, i:high] + contract(x_ref[:, :high], dense_ref[i:high, :high])


def on_odd_segment():
    return lax.rem(lax.axis_index("seg"), 2) == 1


def choose_kernel(own_ref, far_ref, o_ref):
    @pl.when(on_odd_segment())
    def _():
        o_ref[...] = own_ref[...]

    @pl.when(jnp.logical_not(on_odd_segment()))
    def _():
        o_ref[...] = far_ref[...]


def near_kernel(x_ref, low_near_ref, low_far_ref, dense_ref, total_ref, o_ref, wide):
    m = x_ref.shape[1]
    half = m // 2
    depth = 256
    for i in range(0, m, depth):
        lanes = pl.ds(i, depth)
        total = total_ref[:, lanes] + low_near_ref[:, lanes].astype(F32) + low_far_ref[:, lanes].astype(F32)
        wide[:, lanes] = total + contract(x_ref[...], dense_ref[lanes, :])
        for t in range(0, 16, 2):
            parts = [wide[12 * u : 12 * u + 8, lanes] for u in (t, t + 1)]
            o_ref[8 * t : 8 * t + 16, lanes] = jnp.concatenate(parts, 0).astype(BF16)
        if i >= half:
            for t in range(0, 16, 2):
                parts = [
                    wide[12 * u + 8 : 12 * u + 12, pl.ds(k, depth)] for u in (t, t + 1) for k in (i - half, i)
                ]
                o_ref[8 * t : 8 * t + 16, pl.ds(half + i, depth)] = jnp.concatenate(parts, 0).astype(BF16)


def call(kernel, name, outs, mib, *args, scratch=(), flops=0, far_off=(), far_out=False):
    several = isinstance(outs, tuple)
    size = sum(a.size * a.dtype.itemsize for a in args)
    in_specs = vmem_specs(len(args))
    for k in far_off:
        in_specs[k] = pl.BlockSpec(memory_space=pltpu.HBM)
    out_spec = pl.BlockSpec(memory_space=pltpu.HBM if far_out else pltpu.VMEM)
    return pl.pallas_call(
        kernel,
        out_shape=outs,
        in_specs=in_specs,
        out_specs=tuple(vmem_specs(len(outs))) if several else out_spec,
        scratch_shapes=list(scratch),
        compiler_params=params(mib),
        cost_estimate=pl.CostEstimate(flops=flops, bytes_accessed=size, transcendentals=0),
        name=name,
    )(*args)


def passed_along(shard, by):
    length, places = lax.axis_size("seg"), lax.axis_size("trait")
    pairs = []
    for s in range(length):
        for p in range(places):
            if 0 <= s + by < length:
                pairs.append((s * places + p, (s + by) * places + (swapped(p) if by % 2 else p)))
    return lax.ppermute(shard, ("seg", "trait"), pairs)


def traded(shard):
    length, places = lax.axis_size("seg"), lax.axis_size("trait")
    pairs = [(s * places + p, (s ^ 1) * places + swapped(p)) for s in range(length) for p in range(places)]
    return lax.ppermute(shard, ("seg", "trait"), pairs)


def exchange(packed):
    rows, lanes = packed.shape
    moved = lax.all_to_all(packed.reshape(16, rows // 16, lanes), "trait", 0, 0, tiled=True)
    return moved.reshape(rows, lanes)


def local(effects, precision, band):
    chains, traits, m = effects.shape
    width = band.shape[1]
    rows = chains * traits
    packed_shape = (8 * chains, m + m // 2)
    struct = jax.ShapeDtypeStruct

    flat = effects.transpose(1, 0, 2).reshape(rows, m)
    packed = call(
        pack_kernel, "pack", struct(packed_shape, BF16), 63, flat,
        far_off=(0,), far_out=True,
        scratch=[
            pltpu.VMEM((rows, m), BF16),
            pltpu.VMEM((m // LANES, rows, LANES), F32),
            pltpu.VMEM(packed_shape, BF16),
            pltpu.SemaphoreType.DMA((4,)),
            pltpu.SemaphoreType.DMA((8,)),
        ],
    )
    square = struct((m, m), BF16)
    within, following, last = call(
        skew_kernel, "skew", (square, square, square), 16, band, flops=m * width
    )
    thin = struct((rows, m), BF16)
    matrices = struct((2, rows, 256), BF16)
    upper, lower = call(weights_kernel, "weights", (matrices, matrices), 16, precision, flops=rows * rows)
    gathered, following = lax.optimization_barrier((exchange(packed), following))
    mixed = call(mix_kernel, "mix", thin, 16, gathered, upper, lower, flops=4 * rows * rows * m)
    far = passed_along(mixed, -2)
    low_near = call(lower_near_kernel, "lower_near", thin, 16, mixed, following, flops=2 * rows * m * m)
    low_near = passed_along(low_near, 1)
    low_far = call(lower_far_kernel, "lower_far", thin, 16, mixed, last, flops=rows * m * m)
    low_far = passed_along(low_far, 2)
    near = traded(call(choose_kernel, "choose", thin, 8, mixed, far))
    wide = struct((rows, m), F32)
    total = call(own_kernel, "own", wide, 16, mixed, within, flops=4 * rows * m * m)
    total = call(far_kernel, "far", wide, 16, far, last, total, flops=rows * m * m)
    packed = call(
        near_kernel, "near", struct(packed_shape, BF16), 16, near, low_near, low_far, following, total,
        flops=2 * rows * m * m, scratch=[pltpu.VMEM((rows, m), F32)],
    )
    flat = call(
        unpack_kernel, "unpack", thin, 8, exchange(packed), far_out=True,
        scratch=[
            pltpu.VMEM((packed_shape[1] // LANES, packed_shape[0], LANES), F32),
            pltpu.VMEM((rows, m), BF16),
            pltpu.SemaphoreType.DMA((4,)),
        ],
    )
    return flat.reshape(traits, chains, m).transpose(1, 0, 2)


def solution(mesh):
    in_specs = (P(None, "trait", "seg"), P(), P("seg", None))
    out_specs = P(None, "trait", "seg")
    return jax.shard_map(local, mesh=mesh, in_specs=in_specs, out_specs=out_specs, check_vma=False)
```

```python
import jax
import jax.numpy as jnp
from jax import lax
from jax.experimental import pallas as pl
from jax.experimental.pallas import tpu as pltpu
from jax.sharding import PartitionSpec as P

F32 = jnp.float32
BF16 = jnp.bfloat16
LANES = 128
MIB = 1 << 20


def vmem_specs(count):
    return [pl.BlockSpec(memory_space=pltpu.VMEM)] * count


def params(mib):
    return pltpu.CompilerParams(vmem_limit_bytes=mib * MIB)


def swapped(place):
    return 8 * (place % 2) + 2 * (place // 2 % 4) + place // 8


def chain_places():
    odd = lax.rem(lax.axis_index("seg"), 2) == 1
    return [jnp.where(odd, swapped(p), p) for p in range(16)]


def pack_kernel(x_ref, o_ref, near, wide, packed, in_sems, out_sems):
    rows, m = x_ref.shape
    blocks = m // LANES
    chunks = in_sems.shape[0]
    part = m // chunks
    chains = chain_places()
    copies = []
    for q in range(chunks):
        lanes = pl.ds(q * part, part)
        copies.append(pltpu.make_async_copy(x_ref.at[:, lanes], near.at[:, lanes], in_sems.at[q]))
        copies[-1].start()
    out = []

    def send(first, size):
        lanes = pl.ds(first, size)
        out.append(pltpu.make_async_copy(packed.at[:, lanes], o_ref.at[:, lanes], out_sems.at[len(out)]))
        out[-1].start()

    for q in range(chunks):
        copies[q].wait()
        for k in range(q * blocks // chunks, (q + 1) * blocks // chunks):
            wide[k] = near[:, k * LANES : (k + 1) * LANES].astype(F32)
            for p in range(0, 16, 2):
                parts = [wide[k, pl.ds(d, 8, stride=16), :] for d in chains[p : p + 2]]
                packed[8 * p : 8 * p + 16, k * LANES : (k + 1) * LANES] = jnp.concatenate(parts, 0).astype(BF16)
        send(q * part, part)
    for p in range(0, 16, 2):
        for k in range(blocks // 2):
            parts = [
                wide[k + h, pl.ds(128 + d, 4, stride=16), :]
                for d in chains[p : p + 2]
                for h in (0, blocks // 2)
            ]
            packed[8 * p : 8 * p + 16, m + k * LANES : m + (k + 1) * LANES] = jnp.concatenate(parts, 0).astype(BF16)
    send(m, m // 2)
    for copy in out:
        copy.wait()


def unpack_kernel(x_ref, o_ref, wide, held, sems):
    m = o_ref.shape[1]
    blocks = m // LANES
    chunks = sems.shape[0]
    chains = chain_places()

    def widen(k):
        for p in range(0, 16, 2):
            pair = x_ref[8 * p : 8 * p + 16, k * LANES : (k + 1) * LANES].astype(F32)
            for h in range(2):
                wide[k, pl.ds(pl.multiple_of(8 * chains[p + h], 8), 8), :] = pair[8 * h : 8 * h + 8]

    for k in range(blocks, wide.shape[0]):
        widen(k)
    copies = []
    for q in range(chunks):
        for k in range(q * blocks // chunks, (q + 1) * blocks // chunks):
            widen(k)
            lanes = pl.ds(k * LANES, LANES)
            for j in range(8):
                held[16 * j : 16 * j + 16, lanes] = wide[k, pl.ds(j, 16, stride=8), :].astype(BF16)
            half, place = divmod(k, blocks // 2)
            for j in range(4):
                tail = wide[blocks + place, pl.ds(j + 4 * half, 16, stride=8), :]
                held[128 + 16 * j : 144 + 16 * j, lanes] = tail.astype(BF16)
        lanes = pl.ds(q * (m // chunks), m // chunks)
        copies.append(pltpu.make_async_copy(held.at[:, lanes], o_ref.at[:, lanes], sems.at[q]))
        copies[-1].start()
    for copy in copies:
        copy.wait()


def mix_kernel(x_ref, p_ref, o_ref):
    m = o_ref.shape[1]
    half = m // 2
    blank = jnp.zeros((4, p_ref.shape[1]), F32)
    heads, lows, highs = [], [], []
    for t in range(16):
        heads.append(p_ref[12 * t : 12 * t + 8, :])
        tail = p_ref[12 * t + 8 : 12 * t + 12, :]
        lows += [tail, blank]
        highs += [blank, tail]
    head = jnp.concatenate(heads, 0)
    for first, tails in ((0, lows), (half, highs)):
        weights = jnp.concatenate([head, jnp.concatenate(tails, 0)], 0).T
        upper = weights.astype(BF16)
        lower = (weights - upper.astype(F32)).astype(BF16)
        values = jnp.concatenate([x_ref[:, first : first + half], x_ref[:, m:]], 0)
        total = jnp.dot(upper, values, preferred_element_type=F32)
        total += jnp.dot(lower, values, preferred_element_type=F32)
        o_ref[:, first : first + half] = total.astype(BF16)

def lower_near_kernel(x_ref, dense_ref, o_ref):
    o_ref[...] = jnp.dot(x_ref[...], dense_ref[...], preferred_element_type=F32).astype(BF16)


def lower_far_kernel(x_ref, dense_ref, o_ref):
    depth = 256
    for i in range(0, x_ref.shape[1], depth):
        part = jnp.dot(x_ref[:, i:], dense_ref[i:, i : i + depth], preferred_element_type=F32)
        o_ref[:, i : i + depth] = part.astype(BF16)


def skew_rows(band_ref, dense_refs, first):
    m, width = band_ref.shape
    rows = pl.ds(first, LANES)

    def put(col, tile):
        if col < m + width:
            dense_refs[col // m][rows, pl.ds(col % m, LANES)] = tile

    a = lax.broadcasted_iota(jnp.int32, (LANES, LANES), 0)
    b = lax.broadcasted_iota(jnp.int32, (LANES, LANES), 1)
    ahead = b > a
    zero = jnp.zeros((LANES, LANES), F32)
    before = zero
    for d in range(width // LANES + 1):
        if d < width // LANES:
            tile = band_ref[rows, d * LANES : (d + 1) * LANES].astype(F32)
            now = pltpu.roll(tile, 1, 1, stride=1, stride_axis=0)
        else:
            now = zero
        put(first + d * LANES, jnp.where(ahead, now, before).astype(BF16))
        before = now
    if first % 256:
        put(first - LANES, zero.astype(BF16))
    else:
        put(first + width + LANES, zero.astype(BF16))


def skew_kernel(band_ref, within_ref, following_ref, last_ref, band, within, last, in_sems, out_sems):
    chunks = in_sems.shape[0]
    part = band_ref.shape[0] // chunks
    fetches = []
    for q in range(chunks):
        some = pl.ds(q * part, part)
        fetches.append(pltpu.make_async_copy(band_ref.at[some], band.at[some], in_sems.at[q]))
        fetches[-1].start()
    sends = []
    for q in range(chunks):
        fetches[q].wait()
        some = pl.ds(q * part, part)
        for first in range(q * part, (q + 1) * part, LANES):
            skew_rows(band, (within, following_ref, last), first)
        for k, (source, target) in enumerate(((within, within_ref), (last, last_ref))):
            sends.append(pltpu.make_async_copy(source.at[some], target.at[some], out_sems.at[k, q]))
            sends[-1].start()
    for send in sends:
        send.wait()


def contract(values, dense):
    return lax.dot_general(values, dense, (((1,), (1,)), ((), ())), preferred_element_type=F32)


def own_kernel(x_ref, dense_ref, o_ref):
    m = x_ref.shape[1]
    depth = 256
    for i in range(0, m, depth):
        high = i + depth
        total = x_ref[:, i:high].astype(F32)
        total += jnp.dot(x_ref[:, :high], dense_ref[:high, i:high], preferred_element_type=F32)
        total += contract(x_ref[:, i:], dense_ref[i:high, i:m])
        o_ref[:, i:high] = total


def far_kernel(x_ref, dense_ref, total_ref, o_ref):
    m = x_ref.shape[1]
    depth = 256
    for i in range(0, m, depth):
        high = i + depth
        o_ref[:, i:high] = total_ref[:, i:high] + contract(x_ref[:, :high], dense_ref[i:high, :high])


def on_odd_segment():
    return lax.rem(lax.axis_index("seg"), 2) == 1


def choose_kernel(own_ref, far_ref, o_ref):
    @pl.when(on_odd_segment())
    def _():
        o_ref[...] = own_ref[...]

    @pl.when(jnp.logical_not(on_odd_segment()))
    def _():
        o_ref[...] = far_ref[...]


def near_kernel(x_ref, low_near_ref, low_far_ref, dense_ref, total_ref, o_ref, wide):
    m = x_ref.shape[1]
    half = m // 2
    depth = 256
    for i in range(0, m, depth):
        lanes = pl.ds(i, depth)
        total = total_ref[:, lanes] + low_near_ref[:, lanes].astype(F32) + low_far_ref[:, lanes].astype(F32)
        wide[:, lanes] = total + contract(x_ref[...], dense_ref[lanes, :])
        for t in range(0, 16, 2):
            parts = [wide[12 * u : 12 * u + 8, lanes] for u in (t, t + 1)]
            o_ref[8 * t : 8 * t + 16, lanes] = jnp.concatenate(parts, 0).astype(BF16)
        if i >= half:
            for t in range(0, 16, 2):
                parts = [
                    wide[12 * u + 8 : 12 * u + 12, pl.ds(k, depth)] for u in (t, t + 1) for k in (i - half, i)
                ]
                o_ref[8 * t : 8 * t + 16, pl.ds(half + i, depth)] = jnp.concatenate(parts, 0).astype(BF16)


def call(kernel, name, outs, mib, *args, scratch=(), flops=0, far_off=(), far_out=False, far_outs=()):
    several = isinstance(outs, tuple)
    size = sum(a.size * a.dtype.itemsize for a in args)
    in_specs = vmem_specs(len(args))
    for k in far_off:
        in_specs[k] = pl.BlockSpec(memory_space=pltpu.HBM)
    out_specs = vmem_specs(len(outs)) if several else []
    for k in far_outs:
        out_specs[k] = pl.BlockSpec(memory_space=pltpu.HBM)
    out_spec = pl.BlockSpec(memory_space=pltpu.HBM if far_out else pltpu.VMEM)
    return pl.pallas_call(
        kernel,
        out_shape=outs,
        in_specs=in_specs,
        out_specs=tuple(out_specs) if several else out_spec,
        scratch_shapes=list(scratch),
        compiler_params=params(mib),
        cost_estimate=pl.CostEstimate(flops=flops, bytes_accessed=size, transcendentals=0),
        name=name,
    )(*args)


def passed_along(shard, by):
    length, places = lax.axis_size("seg"), lax.axis_size("trait")
    pairs = []
    for s in range(length):
        for p in range(places):
            if 0 <= s + by < length:
                pairs.append((s * places + p, (s + by) * places + (swapped(p) if by % 2 else p)))
    return lax.ppermute(shard, ("seg", "trait"), pairs)


def traded(shard):
    length, places = lax.axis_size("seg"), lax.axis_size("trait")
    pairs = [(s * places + p, (s ^ 1) * places + swapped(p)) for s in range(length) for p in range(places)]
    return lax.ppermute(shard, ("seg", "trait"), pairs)


def exchange(packed):
    rows, lanes = packed.shape
    moved = lax.all_to_all(packed.reshape(16, rows // 16, lanes), "trait", 0, 0, tiled=True)
    return moved.reshape(rows, lanes)


def local(effects, precision, band):
    chains, traits, m = effects.shape
    width = band.shape[1]
    rows = chains * traits
    packed_shape = (8 * chains, m + m // 2)
    struct = jax.ShapeDtypeStruct

    flat = effects.transpose(1, 0, 2).reshape(rows, m)
    packed = call(
        pack_kernel, "pack", struct(packed_shape, BF16), 63, flat,
        far_off=(0,), far_out=True,
        scratch=[
            pltpu.VMEM((rows, m), BF16),
            pltpu.VMEM((m // LANES, rows, LANES), F32),
            pltpu.VMEM(packed_shape, BF16),
            pltpu.SemaphoreType.DMA((4,)),
            pltpu.SemaphoreType.DMA((5,)),
        ],
    )
    square = struct((m, m), BF16)
    within, following, last = call(
        skew_kernel, "skew", (square, square, square), 49, band, flops=m * width,
        far_off=(0,), far_outs=(0, 2),
        scratch=[
            pltpu.VMEM((m, width), BF16),
            pltpu.VMEM((m, m), BF16),
            pltpu.VMEM((m, m), BF16),
            pltpu.SemaphoreType.DMA((4,)),
            pltpu.SemaphoreType.DMA((2, 4)),
        ],
    )
    thin = struct((rows, m), BF16)
    gathered, following = lax.optimization_barrier((exchange(packed), following))
    mixed = call(mix_kernel, "mix", thin, 16, gathered, precision, flops=4 * rows * rows * m)
    far = passed_along(mixed, -2)
    low_near = call(lower_near_kernel, "lower_near", thin, 16, mixed, following, flops=2 * rows * m * m)
    low_near = passed_along(low_near, 1)
    low_far = call(lower_far_kernel, "lower_far", thin, 16, mixed, last, flops=rows * m * m)
    low_far = passed_along(low_far, 2)
    near = traded(call(choose_kernel, "choose", thin, 8, mixed, far))
    wide = struct((rows, m), F32)
    total = call(own_kernel, "own", wide, 16, mixed, within, flops=4 * rows * m * m)
    total = call(far_kernel, "far", wide, 16, far, last, total, flops=rows * m * m)
    packed = call(
        near_kernel, "near", struct(packed_shape, BF16), 16, near, low_near, low_far, following, total,
        flops=2 * rows * m * m, scratch=[pltpu.VMEM((rows, m), F32)],
    )
    flat = call(
        unpack_kernel, "unpack", thin, 8, exchange(packed), far_out=True,
        scratch=[
            pltpu.VMEM((packed_shape[1] // LANES, packed_shape[0], LANES), F32),
            pltpu.VMEM((rows, m), BF16),
            pltpu.SemaphoreType.DMA((4,)),
        ],
    )
    return flat.reshape(traits, chains, m).transpose(1, 0, 2)


def solution(mesh):
    in_specs = (P(None, "trait", "seg"), P(), P("seg", None))
    out_specs = P(None, "trait", "seg")
    return jax.shard_map(local, mesh=mesh, in_specs=in_specs, out_specs=out_specs, check_vma=False)
```
